32 devices in a mesh: seg: 8 (over y, x, core), sec: 4 (over z).
Axes of the slice: x: 2, y: 2, z: 4, core: 2. Of those that a mesh axis runs over, the one named last changes fastest.
Arguments:
- blocks: bfloat16 [8, 4, 4, 128, 128], P('seg', None, 'sec'), may hold values from -0.5 to 0.5
- left_edge: bfloat16 [4, 128], P('sec'), may hold values from -0.5 to 0.5
- right_edge: bfloat16 [4, 128], P('sec'), may hold values from -6 to 6
- occupation: int32 [1024, 8], P(None, 'seg'), may hold values from 0 to 3
- start_sector: int32 [1024], replicated, may hold values from 0 to 3
Outputs:
- amplitude: float32 [1024], replicated
The draws below stay inside these ranges and needn't reach their ends.
All inputs are finite; a program needn't handle non-finite values.
Results may differ from the reference program's by a relative error of at most 0.015.
Values may be sent and summed in bfloat16 or wider, within the bound.
A program may use at most 64 MiB of HBM per device.

```python
import jax
import jax.numpy as jnp

SW = 128
NSEC = 4
LOCAL = 4
SITES = 8
MID = 4
CONF = 1024


def plant(drawn, rng, low, high):
    shape = drawn.shape
    place = [jax.random.randint(jax.random.fold_in(rng, axis), (), 0, shape[axis]) for axis in range(len(shape))]
    drawn = drawn.at[tuple(place)].set(low)
    longest = shape.index(max(shape))
    place[longest] = (place[longest] + 1) % shape[longest]
    return drawn.at[tuple(place)].set(high)


def shard_levels(own_key, extent, pieces, least, top_value):
    factor_of = 1.0
    for position, shards_of in pieces:
        draws = jax.random.uniform(jax.random.fold_in(jax.random.fold_in(own_key, 6), position), (shards_of,), jnp.float32, least / len(pieces), top_value / len(pieces))
        factor_of = factor_of * jnp.repeat(jnp.exp(draws), extent[position] // shards_of).reshape((-1,) + (1,) * (len(extent) - 1 - position))
    return factor_of


def gaussian(rng, extent, deviation, most, split=(), held_as=jnp.bfloat16):
    values = deviation * jax.random.normal(rng, extent, jnp.float32)
    if split:
        values = values * shard_levels(rng, extent, split, -0.22, 0.18)
    return jnp.clip(values, -most, most).astype(held_as)


def setup_inputs(seed: int = 0) -> dict:
    seeds = jax.random.split(jax.random.key(seed), 6)
    blocks = gaussian(seeds[0], (SITES, LOCAL, NSEC, SW, SW), SW ** -0.5, 0.5, ((0, 8), (2, 4)))
    left_edge = gaussian(seeds[1], (NSEC, SW), SW ** -0.5, 0.5, ((0, 4),))
    right_edge = gaussian(seeds[2], (NSEC, SW), 1.0, 6.0, ((0, 4),))
    occupation = plant(jax.random.randint(seeds[3], (CONF, SITES), 0, 4), jax.random.fold_in(seeds[3], 1), 0, 3).astype(jnp.int32)
    start_sector = plant(jax.random.randint(seeds[4], (CONF,), 0, NSEC), jax.random.fold_in(seeds[4], 1), 0, NSEC - 1).astype(jnp.int32)
    return dict(blocks=blocks, left_edge=left_edge, right_edge=right_edge, occupation=occupation, start_sector=start_sector)


def reference(blocks, left_edge, right_edge, occupation, start_sector):
    charge = jnp.array([0, 1, -1, 0], dtype=jnp.int32)
    charge_step = charge[occupation]
    running = jnp.cumsum(charge_step, axis=1).astype(jnp.int32)
    first_col = jnp.zeros((occupation.shape[0], 1), dtype=jnp.int32)
    sector = (start_sector[:, None] + jnp.concatenate([first_col, running], axis=1)) % NSEC
    sector = sector.astype(jnp.int32)
    left_env = left_edge[sector[:, 0]]
    for site_index in range(MID):
        chosen = blocks[site_index][occupation[:, site_index], sector[:, site_index]]
        left_env = jnp.einsum("ka,kab->kb", left_env.astype(jnp.float32), chosen.astype(jnp.float32)).astype(jnp.bfloat16)
    right_env = right_edge[sector[:, SITES]]
    for site_index in range(SITES - 1, MID - 1, -1):
        chosen = blocks[site_index][occupation[:, site_index], sector[:, site_index]]
        right_env = jnp.einsum("kab,kb->ka", chosen.astype(jnp.float32), right_env.astype(jnp.float32)).astype(jnp.bfloat16)
    return jnp.sum(left_env.astype(jnp.float32) * right_env.astype(jnp.float32), axis=1)
```

```python
import functools

import jax
import jax.numpy as jnp
from jax import lax
from jax.experimental import pallas as pl
from jax.experimental.pallas import tpu as pltpu
from jax.sharding import PartitionSpec as P

MESH = pl.DeviceIdType.MESH
SLOTS = (0, 3, 1, 2)


def tree_kernel(
    seg_count, sec_count,
    blocks_hbm, left_ref, right_ref, occ_ref, start_ref, out_ref,
    mats, x_in, y_out, big_out, l_in, r_in, occ_in, one_l, one_r, sel_r, fin,
    mat_sem, ch_send, ch_recv, l_recv, occ_send, occ_recv, fin_send, fin_recv,
):
    seg = lax.axis_index("seg")
    sec = lax.axis_index("sec")
    up = lax.rem(sec + 1, sec_count)
    down = lax.rem(sec + sec_count - 1, sec_count)
    half = seg_count // 2
    last = seg_count - 1
    near = (sec, up, down)
    hub = half

    load = pltpu.make_async_copy(blocks_hbm, mats, mat_sem)
    load.start()

    barrier = pltpu.get_barrier_semaphore()

    def greet(seg_to, sec_to):
        pl.semaphore_signal(barrier, inc=1, device_id=(seg_to, sec_to), device_id_type=MESH)

    @pl.when(seg == hub)
    def _():
        for i in range(seg_count):
            if i != hub:
                greet(i, sec)
        for i in (hub - 1, hub + 1):
            greet(i, up)
            greet(i, down)
        for step in range(1, sec_count):
            greet(hub, lax.rem(sec + step, sec_count))

    @pl.when(seg != hub)
    def _():
        @pl.when(jnp.logical_and(seg >= 1, seg < last))
        def _():
            before = jnp.where(seg < half, seg - 1, seg + 1)
            for place in near:
                greet(before, place)

        @pl.when(seg == last)
        def _():
            greet(last, up)
            greet(last, down)

        for place in range(sec_count):
            greet(hub, place)

    def send(src, dst, send_sem, recv_sem, seg_to, sec_to):
        copy = pltpu.make_async_remote_copy(
            src_ref=src, dst_ref=dst, send_sem=send_sem, recv_sem=recv_sem,
            device_id=(seg_to, sec_to), device_id_type=MESH,
        )
        copy.start()
        return copy

    def arrived(dst, recv_sem):
        pltpu.make_async_remote_copy(
            src_ref=dst, dst_ref=dst, send_sem=ch_send.at[0], recv_sem=recv_sem,
            device_id=(seg, sec), device_id_type=MESH,
        ).wait_recv()

    def send_occ():
        return send(occ_ref, occ_in.at[seg], occ_send, occ_recv.at[seg], hub, sec)

    rows16 = lax.broadcasted_iota(jnp.int32, (16, 128), 0)

    def pick(index, parts):
        total = parts[3]
        for n in (2, 1, 0):
            total = jnp.where(index == n, parts[n], total)
        return total

    def left_products(x):
        return [
            jnp.dot(x, mats[n], preferred_element_type=jnp.float32).astype(jnp.bfloat16)
            for n in SLOTS
        ]

    def left_send(out, into, sems):
        return (
            send(out.at[0:2], into.at[0:2], ch_send.at[0], sems.at[0], seg + 1, sec),
            send(out.at[2:3], into.at[2:3], ch_send.at[1], sems.at[1], seg + 1, up),
            send(out.at[3:4], into.at[3:4], ch_send.at[2], sems.at[2], seg + 1, down),
        )

    def left_wait(into, sems):
        arrived(into.at[0:2], sems.at[0])
        arrived(into.at[2:3], sems.at[1])
        arrived(into.at[3:4], sems.at[2])

    def left_slots():
        by_n = [None] * 4
        for place, n in enumerate(SLOTS):
            by_n[n] = x_in[place]
        return by_n

    def f32(parts):
        return [part.astype(jnp.float32) for part in parts]

    def right_products(parts):
        return [
            lax.dot_general(
                parts[place], mats[n], (((1,), (1,)), ((), ())),
                preferred_element_type=jnp.float32,
            )
            for n, place in enumerate((0, 1, 2, 0))
        ]

    def right_send(out, into):
        return (
            send(out, into.at[0], ch_send.at[0], ch_recv.at[0], seg - 1, sec),
            send(out, into.at[2], ch_send.at[1], ch_recv.at[2], seg - 1, up),
            send(out, into.at[1], ch_send.at[2], ch_recv.at[1], seg - 1, down),
        )

    def right_wait(into):
        for place in range(3):
            arrived(into.at[place], ch_recv.at[place])

    def finish(copies):
        for copy in copies:
            copy.wait_send()

    def edge_rows(ref):
        return jnp.broadcast_to(ref[...].astype(jnp.float32), (16, 128)).astype(jnp.bfloat16)

    @pl.when(seg == 0)
    def _():
        pl.semaphore_wait(barrier, 4)
        load.wait()
        for place, part in enumerate(left_products(edge_rows(left_ref))):
            y_out[place] = part
        copies = left_send(y_out, x_in, ch_recv)
        occ = send_occ()
        finish(copies + (occ,))

    @pl.when(jnp.logical_or(seg == 1, seg == 2))
    def _():
        pl.semaphore_wait(barrier, 4)
        occ = send_occ()
        load.wait()
        left_wait(x_in, ch_recv)
        index = jnp.where(seg == 1, lax.rem(rows16, 4), lax.div(rows16, 4))
        x = pick(index, f32(left_slots())).astype(jnp.bfloat16)
        for place, part in enumerate(left_products(x)):
            y_out[place] = part
        copies = left_send(y_out, x_in, ch_recv)
        finish(copies + (occ,))

    @pl.when(seg == 3)
    def _():
        pl.semaphore_wait(barrier, 3)
        occ = send_occ()
        load.wait()
        left_wait(x_in, ch_recv)
        x = jnp.concatenate(left_slots(), axis=0)
        for place, part in enumerate(left_products(x)):
            big_out[place] = part
        copies = left_send(big_out, l_in, l_recv)
        finish(copies + (occ,))

    @pl.when(seg == last)
    def _():
        own = edge_rows(right_ref)
        y_out[0] = own
        pl.semaphore_wait(barrier, 6)
        edges = (
            send(y_out.at[0], x_in.at[2], ch_send.at[0], ch_recv.at[2], seg, up),
            send(y_out.at[0], x_in.at[1], ch_send.at[1], ch_recv.at[1], seg, down),
        )
        occ = send_occ()
        load.wait()
        arrived(x_in.at[1], ch_recv.at[1])
        arrived(x_in.at[2], ch_recv.at[2])
        parts = right_products((own, x_in[1], x_in[2]))
        y_out[1] = pick(lax.rem(rows16, 4), parts).astype(jnp.bfloat16)
        finish(edges)
        copies = right_send(y_out.at[1], x_in)
        finish(copies + (occ,))

    @pl.when(seg == 6)
    def _():
        pl.semaphore_wait(barrier, 4)
        occ = send_occ()
        load.wait()
        right_wait(x_in)
        parts = right_products((x_in[0], x_in[1], x_in[2]))
        y_out[0] = pick(lax.div(rows16, 4), parts).astype(jnp.bfloat16)
        copies = right_send(y_out.at[0], x_in)
        finish(copies + (occ,))

    @pl.when(seg == 5)
    def _():
        pl.semaphore_wait(barrier, 3)
        occ = send_occ()
        load.wait()
        right_wait(x_in)
        parts = right_products((x_in[0], x_in[1], x_in[2]))
        for n in range(4):
            big_out[0, n * 16:(n + 1) * 16, :] = parts[n].astype(jnp.bfloat16)
        copies = right_send(big_out.at[0], r_in)
        finish(copies + (occ,))

    @pl.when(seg == hub)
    def _():
        for i in range(seg_count):
            if i != hub:
                arrived(occ_in.at[i], occ_recv.at[i])
        occ = [occ_ref[...] if i == hub else occ_in[i] for i in range(seg_count)]
        middle = start_ref[...]
        for n in occ[:half]:
            middle = middle + jnp.where(n == 1, 1, 0) - jnp.where(n == 2, 1, 0)
        slot = jnp.where(occ[3] == 0, 0, jnp.where(occ[3] == 3, 1, occ[3] + 1))
        key_l = slot * 64 + occ[2] * 16 + occ[1] * 4 + occ[0]
        key_l = jnp.where(lax.rem(middle + 2 * sec_count, sec_count) == sec, key_l, -1)
        key_r = occ[4] * 64 + occ[5] * 16 + occ[6] * 4 + occ[7]
        rows = lax.broadcasted_iota(jnp.int32, (256, 128), 0)
        for j in range(8):
            here = slice(j * 128, (j + 1) * 128)
            one_r[:, here] = jnp.where(rows == key_r[j:j + 1, :], 1.0, 0.0).astype(jnp.bfloat16)
            one_l[:, here] = jnp.where(rows == key_l[j:j + 1, :], 1.0, 0.0).astype(jnp.bfloat16)
        load.wait()

        def select(vectors, one_hot):
            return lax.dot_general(
                vectors, one_hot[...], (((0,), (0,)), ((), ())),
                preferred_element_type=jnp.float32,
            )

        right_wait(r_in)
        parts = right_products((r_in[0], r_in[1], r_in[2]))
        right = jnp.concatenate([part.astype(jnp.bfloat16) for part in parts], axis=0)
        sel_r[...] = select(right, one_r)
        left_wait(l_in, l_recv)
        left = jnp.concatenate([l_in[place] for place in range(4)], axis=0)
        value = jnp.sum(select(left, one_l) * sel_r[...], axis=0, keepdims=True)
        for j in range(8):
            fin[sec, j:j + 1, :] = value[:, j * 128:(j + 1) * 128]
        count = seg_count * sec_count
        pl.semaphore_wait(barrier, count - 1)
        me = seg * sec_count + sec
        copies = []
        for step in range(1, count):
            to = lax.rem(me + step, count)
            copies.append(
                send(
                    fin.at[sec], fin.at[sec], fin_send.at[step - 1], fin_recv.at[sec],
                    lax.div(to, sec_count), lax.rem(to, sec_count),
                )
            )
        finish(copies)

    for place in range(sec_count):
        @pl.when(jnp.logical_or(seg != hub, sec != place))
        def _():
            arrived(fin.at[place], fin_recv.at[place])

    out_ref[...] = (fin[0] + fin[1]) + (fin[2] + fin[3])


def tree_device(blocks, left_edge, right_edge, occupation, start_sector):
    seg_count = lax.axis_size("seg")
    sec_count = lax.axis_size("sec")
    vmem = pl.BlockSpec(memory_space=pltpu.VMEM)
    dma = pltpu.SemaphoreType.DMA
    bf16, f32, i32 = jnp.bfloat16, jnp.float32, jnp.int32
    values = pl.pallas_call(
        functools.partial(tree_kernel, seg_count, sec_count),
        out_shape=jax.ShapeDtypeStruct((8, 128), f32),
        in_specs=[pl.BlockSpec(memory_space=pl.ANY)] + [vmem] * 4,
        out_specs=vmem,
        scratch_shapes=[
            pltpu.VMEM((4, 128, 128), bf16),
            pltpu.VMEM((4, 16, 128), bf16),
            pltpu.VMEM((4, 16, 128), bf16),
            pltpu.VMEM((4, 64, 128), bf16),
            pltpu.VMEM((4, 64, 128), bf16),
            pltpu.VMEM((3, 64, 128), bf16),
            pltpu.VMEM((8, 8, 128), i32),
            pltpu.VMEM((256, 1024), bf16),
            pltpu.VMEM((256, 1024), bf16),
            pltpu.VMEM((128, 1024), f32),
            pltpu.VMEM((4, 8, 128), f32),
            dma,
            dma((3,)),
            dma((3,)),
            dma((3,)),
            dma,
            dma((8,)),
            dma((seg_count * sec_count - 1,)),
            dma((4,)),
        ],
        compiler_params=pltpu.CompilerParams(
            collective_id=0, has_side_effects=True, vmem_limit_bytes=16 * 1024 * 1024
        ),
    )(
        blocks.reshape(4, 128, 128),
        left_edge,
        right_edge,
        occupation.reshape(8, 128),
        start_sector.reshape(8, 128),
    )
    return values.reshape(1024)


def fits_tree(mesh, blocks, occupation):
    seg_count, sec_count = mesh.shape["seg"], mesh.shape["sec"]
    return (
        seg_count == 8
        and sec_count == 4
        and blocks.shape == (8, 4, 4, 128, 128)
        and occupation.shape == (1024, 8)
    )


def padded_2(block, sides, width, periodic):
    for axis, dim in sides:
        count = lax.axis_size(axis)
        forward = [(i, i + 1) for i in range(count - 1)]
        if periodic:
            forward.append((count - 1, 0))
        backward = [(target, source) for source, target in forward]
        low = lax.ppermute(
            lax.slice_in_dim(block, block.shape[dim] - width, None, axis=dim), axis, forward
        )
        high = lax.ppermute(lax.slice_in_dim(block, 0, width, axis=dim), axis, backward)
        block = jnp.concatenate([low, block, high], axis=dim)
    return block


def state_masks(occ_site):
    levels = jnp.arange(4, dtype=jnp.int32)
    return (occ_site[:, None] == levels[None, :]).astype(jnp.float32)


def forward_send(vector, block_site, occ_masks):
    products = jnp.einsum("ka,nab->knb", vector, block_site, preferred_element_type=jnp.float32)
    terms = products * occ_masks[:, :, None]
    kept_term = (terms[:, 0] + terms[:, 3]).astype(jnp.bfloat16)
    upward = terms[:, 1].astype(jnp.bfloat16)
    downward = terms[:, 2].astype(jnp.bfloat16)
    return (kept_term, jnp.stack([downward, upward]))


def backward_send(vector, block_site, occ_masks):
    return (vector, jnp.stack([vector, vector]))


def forward_take(kept_term, padded, block_site, occ_masks):
    total = (
        kept_term.astype(jnp.float32)
        + padded[0].astype(jnp.float32)
        + padded[3].astype(jnp.float32)
    )
    return total.astype(jnp.bfloat16)


def backward_take(kept_term, padded, block_site, occ_masks):
    stacked = jnp.stack([kept_term, padded[3], padded[0], kept_term], axis=1)
    products = jnp.einsum("nab,knb->kna", block_site, stacked, preferred_element_type=jnp.float32)
    return jnp.sum(products * occ_masks[:, :, None], axis=1).astype(jnp.bfloat16)


def per_device(blocks, left_edge, right_edge, occupation, start_sector):
    seg_count = lax.axis_size("seg")
    half_count = seg_count // 2
    seg_index = lax.axis_index("seg")
    sec_index = lax.axis_index("sec")
    is_left = seg_index < half_count
    chain_depth = jnp.where(is_left, seg_index, seg_count - 1 - seg_index)
    is_first = chain_depth == 0
    meet_lower = seg_index == half_count - 1
    meet_upper = seg_index == half_count
    conf_count = occupation.shape[0]
    sites_here = occupation.shape[1]
    sector_width = blocks.shape[-1]
    block_count = 1
    columns = jnp.arange(sector_width, dtype=jnp.int32)
    lower_cols = (columns < sector_width // 2).astype(jnp.float32)
    upper_cols = 1.0 - lower_cols
    local_blocks = blocks[:, :, 0]
    left_row = left_edge[0]
    right_row = right_edge[0]
    batch_rows = conf_count // block_count

    def initial():
        zero_row = jnp.zeros_like(left_row)
        initial_left = jnp.where(
            (start_sector == sec_index)[:, None], left_row[None, :], zero_row[None, :]
        )
        initial_right = jnp.broadcast_to(right_row[None, :], (batch_rows, sector_width))
        return jnp.where(is_left, initial_left, initial_right)

    def run_sites(vector):
        position = jnp.where(is_left, 0, sites_here - 1)
        block_site = lax.dynamic_index_in_dim(local_blocks, position, 0, keepdims=False)
        occ_site = lax.dynamic_index_in_dim(occupation, position, 1, keepdims=False)
        occ_masks = state_masks(occ_site)
        kept_term, outgoing = lax.cond(
            is_left, forward_send, backward_send, vector, block_site, occ_masks
        )
        padded = padded_2(outgoing, (("sec", 0),), 1, True)
        vector = lax.cond(
            is_left, forward_take, backward_take, kept_term, padded, block_site, occ_masks
        )
        return vector

    section_count = half_count + block_count - 1

    def section(section_index, state_pair):
        incoming, partial_value = state_pair
        batch_index = section_index - chain_depth
        is_valid = (batch_index >= 0) & (batch_index < block_count)
        vector = jnp.where(is_first, initial(), incoming)
        vector = run_sites(vector)
        padded = padded_2(vector[None], (("seg", 0),), 1, False)
        received = jnp.where(is_left, padded[0], padded[2])
        own_vals = vector.astype(jnp.float32)
        lower_part = jnp.sum(own_vals * padded[2].astype(jnp.float32) * lower_cols[None, :], axis=1)
        upper_part = jnp.sum(own_vals * padded[0].astype(jnp.float32) * upper_cols[None, :], axis=1)
        product = jnp.where(meet_lower, lower_part, upper_part)
        previous = partial_value
        store_here = (meet_lower | meet_upper) & is_valid
        partial_value = jnp.where(store_here, product, previous)
        return (received, partial_value)

    start_state = (
        jnp.zeros((batch_rows, sector_width), jnp.bfloat16),
        jnp.zeros((conf_count,), jnp.float32),
    )
    final_state = lax.fori_loop(0, section_count, section, start_state)
    return lax.psum(final_state[1], ("seg", "sec"))


def solution(mesh):
    in_specs = (
        P("seg", None, "sec", None, None),
        P("sec", None),
        P("sec", None),
        P(None, "seg"),
        P(),
    )

    def run(blocks, left_edge, right_edge, occupation, start_sector):
        body = tree_device if fits_tree(mesh, blocks, occupation) else per_device
        return jax.shard_map(
            body, mesh=mesh, in_specs=in_specs, out_specs=P(), check_vma=False
        )(blocks, left_edge, right_edge, occupation, start_sector)

    return run
```

```python
import functools

import jax
import jax.numpy as jnp
from jax import lax
from jax.experimental import pallas as pl
from jax.experimental.pallas import tpu as pltpu
from jax.sharding import PartitionSpec as P

MESH = pl.DeviceIdType.MESH
CHARGE = (0, 1, -1, 0)
SITE2_PIECES = ((0, 0, 4), (1, 0, 1), (1, 2, 4), (2, 1, 3), (3, 0, 2), (3, 3, 4))


def tree_kernel(
    seg_count, sec_count,
    blocks_hbm, left_hbm, right_hbm, occ_hbm, start_hbm, out_ref,
    mats, gath, cross, x_in, z_in, y_out, left_out, left_in,
    edge, occ_in, start_in, one_l, one_r, sel_r, fin,
    load_sem, edge_sem, occ_sem, start_sem, ch_send, ch_recv, z_recv, gath_send, gath_recv,
    l_send, l_recv, occ_send, occ_recv, fin_send, fin_recv,
):
    seg = lax.axis_index("seg")
    sec = lax.axis_index("sec")
    up = lax.rem(sec + 1, sec_count)
    down = lax.rem(sec + sec_count - 1, sec_count)
    half = seg_count // 2
    last = seg_count - 1
    near = (sec, up, down)
    hub = half

    def turned(step):
        return lax.rem(sec + step, sec_count)

    load = pltpu.make_async_copy(blocks_hbm, mats, load_sem)
    barrier = pltpu.get_barrier_semaphore()

    def greet(seg_to, sec_to):
        pl.semaphore_signal(barrier, inc=1, device_id=(seg_to, sec_to), device_id_type=MESH)

    def greet_hubs():
        for step in range(sec_count):
            greet(hub, turned(step))

    def send(src, dst, send_sem, recv_sem, seg_to, sec_to):
        copy = pltpu.make_async_remote_copy(
            src_ref=src, dst_ref=dst, send_sem=send_sem, recv_sem=recv_sem,
            device_id=(seg_to, sec_to), device_id_type=MESH,
        )
        copy.start()
        return copy

    def arrived(dst, recv_sem):
        pltpu.make_async_remote_copy(
            src_ref=dst, dst_ref=dst, send_sem=ch_send.at[0], recv_sem=recv_sem,
            device_id=(seg, sec), device_id_type=MESH,
        ).wait_recv()

    def send_occ():
        return send(occ_hbm, occ_in.at[seg], occ_send, occ_recv.at[seg], hub, sec)

    rows16 = lax.broadcasted_iota(jnp.int32, (16, 128), 0)

    def pick(index, parts):
        total = parts[3]
        for n in (2, 1, 0):
            total = jnp.where(index == n, parts[n], total)
        return total

    def left_mul(x, block):
        return jnp.dot(x, block, preferred_element_type=jnp.float32)

    def right_mul(x, block):
        return lax.dot_general(
            x, block, (((1,), (1,)), ((), ())), preferred_element_type=jnp.float32
        )

    def rounded(x):
        return x.astype(jnp.bfloat16)

    def right_products(parts):
        return [right_mul(parts[place], mats[n]) for n, place in enumerate((0, 1, 2, 0))]

    def to_all(out, seg_to):
        copies = ()
        for step in range(sec_count):
            slot = (sec_count - step) % sec_count
            copies += (
                send(out, z_in.at[slot], ch_send.at[step], z_recv.at[slot], seg_to, turned(step)),
            )
        return copies

    def finish(copies):
        for copy in copies:
            copy.wait_send()

    def edge_load(ref):
        copy = pltpu.make_async_copy(ref, edge, edge_sem)
        copy.start()
        return copy

    def edge_rows():
        return rounded(jnp.broadcast_to(edge[...].astype(jnp.float32), (16, 128)))

    @pl.when(seg == 0)
    def _():
        edges = edge_load(left_hbm)
        load.start()
        greet_hubs()
        edges.wait()
        load.wait()
        x = edge_rows()
        for place, n in enumerate((0, 3, 1, 2)):
            y_out[place] = rounded(left_mul(x, mats[n]))
        pl.semaphore_wait(barrier, 4)
        copies = (
            send(y_out.at[2:3], x_in.at[2:3], ch_send.at[1], ch_recv.at[1], 1, up),
            send(y_out.at[3:4], x_in.at[3:4], ch_send.at[2], ch_recv.at[2], 1, down),
            send(y_out.at[0:2], x_in.at[0:2], ch_send.at[0], ch_recv.at[0], 1, sec),
        )
        occ = send_occ()
        finish(copies + (occ,))

    @pl.when(seg == 1)
    def _():
        for place in near:
            greet(0, place)
        greet_hubs()
        load.start()
        pl.semaphore_wait(barrier, 5)
        occ = send_occ()
        load.wait()
        arrived(x_in.at[0:2], ch_recv.at[0])
        arrived(x_in.at[2:3], ch_recv.at[1])
        arrived(x_in.at[3:4], ch_recv.at[2])
        parts = [x_in[place].astype(jnp.float32) for place in (0, 2, 3, 1)]
        x = rounded(pick(lax.rem(rows16, 4), parts))
        parts = [left_mul(x, mats[n]) for n in range(4)]
        y_out[0] = rounded(pick(lax.div(rows16, 4), parts))
        finish(to_all(y_out.at[0], 3) + (occ,))

    @pl.when(seg == 2)
    def _():
        greet_hubs()
        pl.semaphore_wait(barrier, 5)
        copies = ()
        for place, (turn, low, high) in enumerate(SITE2_PIECES):
            copies += (
                send(
                    blocks_hbm.at[low:high], gath.at[turn, low:high], gath_send.at[place],
                    gath_recv.at[place], 3, turned(sec_count - turn),
                ),
            )
        occ = send_occ()
        finish(copies + (occ,))

    @pl.when(seg == 3)
    def _():
        greet(3, up)
        greet(3, down)
        for step in range(sec_count):
            greet(2, turned(step))
        for step in range(sec_count):
            greet(1, turned(step))
        greet_hubs()
        load.start()
        pl.semaphore_wait(barrier, 3)
        copies = (
            send(blocks_hbm.at[1:2], cross.at[0:1], ch_send.at[0], ch_recv.at[0], 3, up),
            send(blocks_hbm.at[2:3], cross.at[1:2], ch_send.at[1], ch_recv.at[1], 3, down),
        )
        occ = send_occ()
        load.wait()
        arrived(cross.at[0:1], ch_recv.at[0])
        arrived(cross.at[1:2], ch_recv.at[1])
        for place, (turn, low, high) in enumerate(SITE2_PIECES):
            arrived(gath.at[turn, low:high], gath_recv.at[place])
        for slot in range(4):
            arrived(z_in.at[slot], z_recv.at[slot])
        heads = [z_in[slot].astype(jnp.float32) for slot in range(4)]
        block_rows = lax.div(rows16, 4)
        bond2 = [
            rounded(pick(block_rows, [heads[(turn - CHARGE[n]) % 4] for n in range(4)]))
            for turn in range(4)
        ]
        bond3 = {}
        for turn in (0, -1, 1):
            parts = []
            for n in range(4):
                source = (turn - CHARGE[n]) % 4
                parts.append(rounded(left_mul(bond2[source], gath[source, n])))
            bond3[turn] = jnp.concatenate(parts, axis=0)
        blocks3 = (mats[0], cross[0], cross[1], mats[3])
        for n in range(4):
            part = left_mul(bond3[-CHARGE[n]], blocks3[n])
            left_out[n * 64:(n + 1) * 64, :] = rounded(part)
        final = send(left_out, left_in, l_send, l_recv, hub, sec)
        finish(copies + (occ, final))

    @pl.when(seg == last)
    def _():
        edges = edge_load(right_hbm)
        greet(last, up)
        greet(last, down)
        greet_hubs()
        load.start()
        edges.wait()
        own = edge_rows()
        y_out[0] = own
        pl.semaphore_wait(barrier, 6)
        copies = (
            send(y_out.at[0], x_in.at[2], ch_send.at[0], ch_recv.at[2], seg, up),
            send(y_out.at[0], x_in.at[1], ch_send.at[1], ch_recv.at[1], seg, down),
        )
        occ = send_occ()
        load.wait()
        arrived(x_in.at[1], ch_recv.at[1])
        arrived(x_in.at[2], ch_recv.at[2])
        parts = right_products((own, x_in[1], x_in[2]))
        y_out[1] = rounded(pick(lax.rem(rows16, 4), parts))
        finish(copies)
        copies = (
            send(y_out.at[1], x_in.at[2], ch_send.at[1], ch_recv.at[2], seg - 1, up),
            send(y_out.at[1], x_in.at[1], ch_send.at[2], ch_recv.at[1], seg - 1, down),
            send(y_out.at[1], x_in.at[0], ch_send.at[0], ch_recv.at[0], seg - 1, sec),
        )
        finish(copies + (occ,))

    @pl.when(seg == 6)
    def _():
        for place in near:
            greet(last, place)
        greet_hubs()
        load.start()
        pl.semaphore_wait(barrier, 4)
        occ = send_occ()
        load.wait()
        for place in range(3):
            arrived(x_in.at[place], ch_recv.at[place])
        parts = right_products((x_in[0], x_in[1], x_in[2]))
        y_out[0] = rounded(pick(lax.div(rows16, 4), parts))
        finish(to_all(y_out.at[0], hub) + (occ,))

    @pl.when(seg == 5)
    def _():
        greet_hubs()
        pl.semaphore_wait(barrier, 3)
        copies = (
            send(blocks_hbm, gath.at[2], gath_send.at[1], gath_recv.at[2], hub, up),
            send(blocks_hbm, gath.at[1], gath_send.at[2], gath_recv.at[1], hub, down),
            send(blocks_hbm, gath.at[0], gath_send.at[0], gath_recv.at[0], hub, sec),
        )
        occ = send_occ()
        finish(copies + (occ,))

    @pl.when(seg == hub)
    def _():
        for place in near:
            greet(hub + 1, place)
        for i in (0, 1, 2, 3, last):
            greet(i, sec)
        for step in range(sec_count):
            greet(hub + 2, turned(step))
        for step in range(1, sec_count):
            greet(hub, turned(step))
        load.start()
        own_occ = pltpu.make_async_copy(occ_hbm, occ_in.at[hub], occ_sem)
        own_occ.start()
        start = pltpu.make_async_copy(start_hbm, start_in, start_sem)
        start.start()
        own_occ.wait()
        start.wait()
        for i in range(seg_count):
            if i != hub:
                arrived(occ_in.at[i], occ_recv.at[i])
        occ = [occ_in[i] for i in range(seg_count)]
        middle = start_in[...]
        for n in occ[:half]:
            middle = middle + jnp.where(n == 1, 1, 0) - jnp.where(n == 2, 1, 0)
        key_l = occ[3] * 64 + occ[2] * 16 + occ[1] * 4 + occ[0]
        key_l = jnp.where(lax.rem(middle + 2 * sec_count, sec_count) == sec, key_l, -1)
        key_r = occ[4] * 64 + occ[5] * 16 + occ[6] * 4 + occ[7]
        rows = lax.broadcasted_iota(jnp.int32, (256, 128), 0)
        for j in range(8):
            here = slice(j * 128, (j + 1) * 128)
            one_r[:, here] = rounded(jnp.where(rows == key_r[j:j + 1, :], 1.0, 0.0))
            one_l[:, here] = rounded(jnp.where(rows == key_l[j:j + 1, :], 1.0, 0.0))
        load.wait()

        def select(vectors, one_hot):
            return lax.dot_general(
                vectors, one_hot[...], (((0,), (0,)), ((), ())),
                preferred_element_type=jnp.float32,
            )

        for place in range(3):
            arrived(gath.at[place], gath_recv.at[place])
        for slot in range(4):
            arrived(z_in.at[slot], z_recv.at[slot])
        bond6 = [z_in[slot] for slot in range(4)]
        bond5 = []
        for place, turn in enumerate((0, 1, -1)):
            parts = [
                rounded(right_mul(bond6[(turn + CHARGE[n]) % 4], gath[place, n]))
                for n in range(4)
            ]
            bond5.append(jnp.concatenate(parts, axis=0))
        right = jnp.concatenate([rounded(part) for part in right_products(bond5)], axis=0)
        sel_r[...] = select(right, one_r)
        arrived(left_in, l_recv)
        value = jnp.sum(select(left_in[...], one_l) * sel_r[...], axis=0, keepdims=True)
        for j in range(8):
            fin[sec, j:j + 1, :] = value[:, j * 128:(j + 1) * 128]
        count = seg_count * sec_count
        pl.semaphore_wait(barrier, count - 1)
        copies = ()

        def spread(seg_to, sec_to):
            return (
                send(
                    fin.at[sec], fin.at[sec], fin_send.at[len(copies)], fin_recv.at[sec],
                    seg_to, sec_to,
                ),
            )

        for j in range(sec_count):
            place = jnp.where(sec < sec_count // 2, sec_count - 1 - j, j)
            for i in range(seg_count):
                if i != hub:
                    copies += spread(i, place)
            if j > 0:
                copies += spread(hub, turned(j))
        finish(copies)

    for place in range(sec_count):
        @pl.when(jnp.logical_or(seg != hub, sec != place))
        def _():
            arrived(fin.at[place], fin_recv.at[place])

    out_ref[...] = (fin[0] + fin[1]) + (fin[2] + fin[3])


def tree_device(blocks, left_edge, right_edge, occupation, start_sector):
    seg_count = lax.axis_size("seg")
    sec_count = lax.axis_size("sec")
    hbm = pl.BlockSpec(memory_space=pl.ANY)
    dma = pltpu.SemaphoreType.DMA
    bf16, f32, i32 = jnp.bfloat16, jnp.float32, jnp.int32
    values = pl.pallas_call(
        functools.partial(tree_kernel, seg_count, sec_count),
        out_shape=jax.ShapeDtypeStruct((8, 128), f32),
        in_specs=[hbm] * 5,
        out_specs=pl.BlockSpec(memory_space=pltpu.VMEM),
        scratch_shapes=[
            pltpu.VMEM((4, 128, 128), bf16),
            pltpu.VMEM((4, 4, 128, 128), bf16),
            pltpu.VMEM((2, 128, 128), bf16),
            pltpu.VMEM((4, 16, 128), bf16),
            pltpu.VMEM((4, 16, 128), bf16),
            pltpu.VMEM((4, 16, 128), bf16),
            pltpu.VMEM((256, 128), bf16),
            pltpu.VMEM((256, 128), bf16),
            pltpu.VMEM((1, 128), bf16),
            pltpu.VMEM((8, 8, 128), i32),
            pltpu.VMEM((8, 128), i32),
            pltpu.VMEM((256, 1024), bf16),
            pltpu.VMEM((256, 1024), bf16),
            pltpu.VMEM((128, 1024), f32),
            pltpu.VMEM((4, 8, 128), f32),
            dma, dma, dma, dma,
            dma((4,)),
            dma((3,)),
            dma((4,)),
            dma((6,)),
            dma((6,)),
            dma, dma, dma,
            dma((8,)),
            dma((seg_count * sec_count - 1,)),
            dma((4,)),
        ],
        compiler_params=pltpu.CompilerParams(
            collective_id=0, has_side_effects=True, vmem_limit_bytes=60 * 1024 * 1024
        ),
    )(
        blocks.reshape(4, 128, 128),
        left_edge,
        right_edge,
        occupation.reshape(8, 128),
        start_sector.reshape(8, 128),
    )
    return values.reshape(1024)


def fits_tree(mesh, blocks, occupation):
    seg_count, sec_count = mesh.shape["seg"], mesh.shape["sec"]
    return (
        seg_count == 8
        and sec_count == 4
        and blocks.shape == (8, 4, 4, 128, 128)
        and occupation.shape == (1024, 8)
    )


def padded_2(block, sides, width, periodic):
    for axis, dim in sides:
        count = lax.axis_size(axis)
        forward = [(i, i + 1) for i in range(count - 1)]
        if periodic:
            forward.append((count - 1, 0))
        backward = [(target, source) for source, target in forward]
        low = lax.ppermute(
            lax.slice_in_dim(block, block.shape[dim] - width, None, axis=dim), axis, forward
        )
        high = lax.ppermute(lax.slice_in_dim(block, 0, width, axis=dim), axis, backward)
        block = jnp.concatenate([low, block, high], axis=dim)
    return block


def state_masks(occ_site):
    levels = jnp.arange(4, dtype=jnp.int32)
    return (occ_site[:, None] == levels[None, :]).astype(jnp.float32)


def forward_send(vector, block_site, occ_masks):
    products = jnp.einsum("ka,nab->knb", vector, block_site, preferred_element_type=jnp.float32)
    terms = products * occ_masks[:, :, None]
    kept_term = (terms[:, 0] + terms[:, 3]).astype(jnp.bfloat16)
    upward = terms[:, 1].astype(jnp.bfloat16)
    downward = terms[:, 2].astype(jnp.bfloat16)
    return (kept_term, jnp.stack([downward, upward]))


def backward_send(vector, block_site, occ_masks):
    return (vector, jnp.stack([vector, vector]))


def forward_take(kept_term, padded, block_site, occ_masks):
    total = (
        kept_term.astype(jnp.float32)
        + padded[0].astype(jnp.float32)
        + padded[3].astype(jnp.float32)
    )
    return total.astype(jnp.bfloat16)


def backward_take(kept_term, padded, block_site, occ_masks):
    stacked = jnp.stack([kept_term, padded[3], padded[0], kept_term], axis=1)
    products = jnp.einsum("nab,knb->kna", block_site, stacked, preferred_element_type=jnp.float32)
    return jnp.sum(products * occ_masks[:, :, None], axis=1).astype(jnp.bfloat16)


def per_device(blocks, left_edge, right_edge, occupation, start_sector):
    seg_count = lax.axis_size("seg")
    half_count = seg_count // 2
    seg_index = lax.axis_index("seg")
    sec_index = lax.axis_index("sec")
    is_left = seg_index < half_count
    chain_depth = jnp.where(is_left, seg_index, seg_count - 1 - seg_index)
    is_first = chain_depth == 0
    meet_lower = seg_index == half_count - 1
    meet_upper = seg_index == half_count
    conf_count = occupation.shape[0]
    sites_here = occupation.shape[1]
    sector_width = blocks.shape[-1]
    block_count = 1
    columns = jnp.arange(sector_width, dtype=jnp.int32)
    lower_cols = (columns < sector_width // 2).astype(jnp.float32)
    upper_cols = 1.0 - lower_cols
    local_blocks = blocks[:, :, 0]
    left_row = left_edge[0]
    right_row = right_edge[0]
    batch_rows = conf_count // block_count

    def initial():
        zero_row = jnp.zeros_like(left_row)
        initial_left = jnp.where(
            (start_sector == sec_index)[:, None], left_row[None, :], zero_row[None, :]
        )
        initial_right = jnp.broadcast_to(right_row[None, :], (batch_rows, sector_width))
        return jnp.where(is_left, initial_left, initial_right)

    def run_sites(vector):
        position = jnp.where(is_left, 0, sites_here - 1)
        block_site = lax.dynamic_index_in_dim(local_blocks, position, 0, keepdims=False)
        occ_site = lax.dynamic_index_in_dim(occupation, position, 1, keepdims=False)
        occ_masks = state_masks(occ_site)
        kept_term, outgoing = lax.cond(
            is_left, forward_send, backward_send, vector, block_site, occ_masks
        )
        padded = padded_2(outgoing, (("sec", 0),), 1, True)
        vector = lax.cond(
            is_left, forward_take, backward_take, kept_term, padded, block_site, occ_masks
        )
        return vector

    section_count = half_count + block_count - 1

    def section(section_index, state_pair):
        incoming, partial_value = state_pair
        batch_index = section_index - chain_depth
        is_valid = (batch_index >= 0) & (batch_index < block_count)
        vector = jnp.where(is_first, initial(), incoming)
        vector = run_sites(vector)
        padded = padded_2(vector[None], (("seg", 0),), 1, False)
        received = jnp.where(is_left, padded[0], padded[2])
        own_vals = vector.astype(jnp.float32)
        lower_part = jnp.sum(own_vals * padded[2].astype(jnp.float32) * lower_cols[None, :], axis=1)
        upper_part = jnp.sum(own_vals * padded[0].astype(jnp.float32) * upper_cols[None, :], axis=1)
        product = jnp.where(meet_lower, lower_part, upper_part)
        previous = partial_value
        store_here = (meet_lower | meet_upper) & is_valid
        partial_value = jnp.where(store_here, product, previous)
        return (received, partial_value)

    start_state = (
        jnp.zeros((batch_rows, sector_width), jnp.bfloat16),
        jnp.zeros((conf_count,), jnp.float32),
    )
    final_state = lax.fori_loop(0, section_count, section, start_state)
    return lax.psum(final_state[1], ("seg", "sec"))


def solution(mesh):
    in_specs = (
        P("seg", None, "sec", None, None),
        P("sec", None),
        P("sec", None),
        P(None, "seg"),
        P(),
    )

    def run(blocks, left_edge, right_edge, occupation, start_sector):
        body = tree_device if fits_tree(mesh, blocks, occupation) else per_device
        return jax.shard_map(
            body, mesh=mesh, in_specs=in_specs, out_specs=P(), check_vma=False
        )(blocks, left_edge, right_edge, occupation, start_sector)

    return run
```

```python
import functools

import jax
import jax.numpy as jnp
from jax import lax
from jax.experimental import pallas as pl
from jax.experimental.pallas import tpu as pltpu
from jax.sharding import PartitionSpec as P

MESH = pl.DeviceIdType.MESH
CHARGE = (0, 1, -1, 0)
SITE2_PIECES = ((0, 0, 4), (1, 0, 1), (1, 2, 4), (2, 1, 3), (3, 0, 2), (3, 3, 4))


def tree_kernel(
    seg_count, sec_count,
    blocks_hbm, left_hbm, right_hbm, occ_hbm, start_hbm, out_ref,
    mats, gath, cross, x_in, z_in, y_out, left_out, left_in,
    edge, ends, occ_in, start_in, one_l, one_r, sel_r, fin,
    load_sem, edge_sem, occ_sem, start_sem, ch_send, ch_recv, z_recv, gath_send, gath_recv,
    l_send, l_recv, occ_send, occ_recv, fin_send, fin_recv,
):
    seg = lax.axis_index("seg")
    sec = lax.axis_index("sec")
    up = lax.rem(sec + 1, sec_count)
    down = lax.rem(sec + sec_count - 1, sec_count)
    half = seg_count // 2
    last = seg_count - 1
    near = (sec, up, down)
    hub = half

    def turned(step):
        return lax.rem(sec + step, sec_count)

    load = pltpu.make_async_copy(blocks_hbm, mats, load_sem)
    barrier = pltpu.get_barrier_semaphore()

    def greet(seg_to, sec_to):
        pl.semaphore_signal(barrier, inc=1, device_id=(seg_to, sec_to), device_id_type=MESH)

    def greet_hubs():
        for step in range(sec_count):
            greet(hub, turned(step))

    def send(src, dst, send_sem, recv_sem, seg_to, sec_to):
        copy = pltpu.make_async_remote_copy(
            src_ref=src, dst_ref=dst, send_sem=send_sem, recv_sem=recv_sem,
            device_id=(seg_to, sec_to), device_id_type=MESH,
        )
        copy.start()
        return copy

    def arrived(dst, recv_sem):
        pltpu.make_async_remote_copy(
            src_ref=dst, dst_ref=dst, send_sem=ch_send.at[0], recv_sem=recv_sem,
            device_id=(seg, sec), device_id_type=MESH,
        ).wait_recv()

    def send_occ():
        return send(occ_hbm, occ_in.at[seg], occ_send, occ_recv.at[seg], hub, sec)

    rows16 = lax.broadcasted_iota(jnp.int32, (16, 128), 0)

    def pick(index, parts):
        total = parts[3]
        for n in (2, 1, 0):
            total = jnp.where(index == n, parts[n], total)
        return total

    def left_mul(x, block):
        return jnp.dot(x, block, preferred_element_type=jnp.float32)

    def right_mul(x, block):
        return lax.dot_general(
            x, block, (((1,), (1,)), ((), ())), preferred_element_type=jnp.float32
        )

    def rounded(x):
        return x.astype(jnp.bfloat16)

    def right_products(parts):
        return [right_mul(parts[place], mats[n]) for n, place in enumerate((0, 1, 2, 0))]

    def to_all(out, seg_to):
        copies = ()
        for step in range(sec_count):
            slot = (sec_count - step) % sec_count
            copies += (
                send(out, z_in.at[slot], ch_send.at[step], z_recv.at[slot], seg_to, turned(step)),
            )
        return copies

    def finish(copies):
        for copy in copies:
            copy.wait_send()

    def edge_load(ref):
        copy = pltpu.make_async_copy(ref, edge, edge_sem)
        copy.start()
        return copy

    def edge_rows():
        return rounded(jnp.broadcast_to(edge[...].astype(jnp.float32), (16, 128)))

    @pl.when(seg == 0)
    def _():
        edges = edge_load(left_hbm)
        load.start()
        greet_hubs()
        edges.wait()
        load.wait()
        x = edge_rows()
        for place, n in enumerate((0, 3, 1, 2)):
            y_out[place] = rounded(left_mul(x, mats[n]))
        pl.semaphore_wait(barrier, 4)
        copies = (
            send(y_out.at[2:3], x_in.at[2:3], ch_send.at[1], ch_recv.at[1], 1, up),
            send(y_out.at[3:4], x_in.at[3:4], ch_send.at[2], ch_recv.at[2], 1, down),
            send(y_out.at[0:2], x_in.at[0:2], ch_send.at[0], ch_recv.at[0], 1, sec),
        )
        occ = send_occ()
        finish(copies + (occ,))

    @pl.when(seg == 1)
    def _():
        for place in near:
            greet(0, place)
        greet_hubs()
        load.start()
        pl.semaphore_wait(barrier, 5)
        occ = send_occ()
        load.wait()
        arrived(x_in.at[0:2], ch_recv.at[0])
        arrived(x_in.at[2:3], ch_recv.at[1])
        arrived(x_in.at[3:4], ch_recv.at[2])
        parts = [x_in[place].astype(jnp.float32) for place in (0, 2, 3, 1)]
        x = rounded(pick(lax.rem(rows16, 4), parts))
        parts = [left_mul(x, mats[n]) for n in range(4)]
        y_out[0] = rounded(pick(lax.div(rows16, 4), parts))
        finish(to_all(y_out.at[0], 3) + (occ,))

    @pl.when(seg == 2)
    def _():
        greet_hubs()
        pl.semaphore_wait(barrier, 5)
        copies = ()
        for place, (turn, low, high) in enumerate(SITE2_PIECES):
            copies += (
                send(
                    blocks_hbm.at[low:high], gath.at[turn, low:high], gath_send.at[place],
                    gath_recv.at[place], 3, turned(sec_count - turn),
                ),
            )
        occ = send_occ()
        finish(copies + (occ,))

    @pl.when(seg == 3)
    def _():
        greet(3, up)
        greet(3, down)
        for step in range(sec_count):
            greet(2, turned(step))
        for step in range(sec_count):
            greet(1, turned(step))
        greet_hubs()
        load.start()
        pl.semaphore_wait(barrier, 3)
        copies = (
            send(blocks_hbm.at[1:2], cross.at[0:1], ch_send.at[0], ch_recv.at[0], 3, up),
            send(blocks_hbm.at[2:3], cross.at[1:2], ch_send.at[1], ch_recv.at[1], 3, down),
        )
        occ = send_occ()
        load.wait()
        arrived(cross.at[0:1], ch_recv.at[0])
        arrived(cross.at[1:2], ch_recv.at[1])
        for place, (turn, low, high) in enumerate(SITE2_PIECES):
            arrived(gath.at[turn, low:high], gath_recv.at[place])
        for slot in range(4):
            arrived(z_in.at[slot], z_recv.at[slot])
        heads = [z_in[slot].astype(jnp.float32) for slot in range(4)]
        block_rows = lax.div(rows16, 4)
        bond2 = [
            rounded(pick(block_rows, [heads[(turn - CHARGE[n]) % 4] for n in range(4)]))
            for turn in range(4)
        ]
        bond3 = {}
        for turn in (0, -1, 1):
            parts = []
            for n in range(4):
                source = (turn - CHARGE[n]) % 4
                parts.append(rounded(left_mul(bond2[source], gath[source, n])))
            bond3[turn] = jnp.concatenate(parts, axis=0)
        blocks3 = (mats[0], cross[0], cross[1], mats[3])
        for n in range(4):
            part = left_mul(bond3[-CHARGE[n]], blocks3[n])
            left_out[n] = rounded(part)
            copies += (
                send(left_out.at[n], left_in.at[n], l_send.at[n], l_recv.at[n], hub, sec),
            )
        finish(copies + (occ,))

    @pl.when(seg == last)
    def _():
        edges = edge_load(right_hbm)
        for step in range(1, sec_count):
            greet(last, turned(step))
        greet(last - 1, sec)
        greet_hubs()
        load.start()
        edges.wait()
        load.wait()
        own = edge_rows()
        kept = jnp.where(
            lax.rem(rows16, 4) == 0, right_mul(own, mats[0]), right_mul(own, mats[3])
        )
        ends[0, 0] = rounded(kept)
        ends[0, 1] = own
        pl.semaphore_wait(barrier, 7)
        copies = ()
        for step in (2, 1, 3):
            copies += (
                send(
                    ends.at[0], ends.at[sec_count - step], ch_send.at[step],
                    z_recv.at[sec_count - step], seg, turned(step),
                ),
            )
        for place, to in ((1, up), (0, down)):
            copies += (
                send(
                    blocks_hbm.at[1:3], gath.at[place, 1:3], gath_send.at[place],
                    gath_recv.at[place], seg, to,
                ),
            )
        occ = send_occ()
        for slot in range(1, 4):
            arrived(ends.at[slot], z_recv.at[slot])
        arrived(gath.at[2], gath_recv.at[2])
        for place in range(2):
            arrived(gath.at[place, 1:3], gath_recv.at[place])
        bond7 = []
        for turn, ones, twos in (
            (0, mats[1], mats[2]), (1, gath[0, 1], gath[0, 2]), (-1, gath[1, 1], gath[1, 2])
        ):
            kept = ends[turn % 4, 0].astype(jnp.float32)
            parts = [
                kept,
                right_mul(ends[(turn + 1) % 4, 1], ones),
                right_mul(ends[(turn - 1) % 4, 1], twos),
                kept,
            ]
            bond7.append(rounded(pick(lax.rem(rows16, 4), parts)))
        parts = [right_mul(bond7[place], gath[2, n]) for n, place in enumerate((0, 1, 2, 0))]
        y_out[0] = rounded(pick(lax.div(rows16, 4), parts))
        finish(copies)
        finish(to_all(y_out.at[0], hub) + (occ,))

    @pl.when(seg == 6)
    def _():
        greet_hubs()
        pl.semaphore_wait(barrier, 2)
        copy = send(blocks_hbm, gath.at[2], gath_send.at[0], gath_recv.at[2], last, sec)
        occ = send_occ()
        finish((copy, occ))

    @pl.when(seg == 5)
    def _():
        greet_hubs()
        pl.semaphore_wait(barrier, 3)
        copies = (
            send(blocks_hbm, gath.at[2], gath_send.at[1], gath_recv.at[2], hub, up),
            send(blocks_hbm, gath.at[1], gath_send.at[2], gath_recv.at[1], hub, down),
            send(blocks_hbm, gath.at[0], gath_send.at[0], gath_recv.at[0], hub, sec),
        )
        occ = send_occ()
        finish(copies + (occ,))

    @pl.when(seg == hub)
    def _():
        for place in near:
            greet(hub + 1, place)
        for i in (0, 1, 2, 3, last - 1):
            greet(i, sec)
        for step in range(sec_count):
            greet(last, turned(step))
        for step in range(1, sec_count):
            greet(hub, turned(step))
        load.start()
        own_occ = pltpu.make_async_copy(occ_hbm, occ_in.at[hub], occ_sem)
        own_occ.start()
        start = pltpu.make_async_copy(start_hbm, start_in, start_sem)
        start.start()
        own_occ.wait()
        start.wait()
        for i in range(seg_count):
            if i != hub:
                arrived(occ_in.at[i], occ_recv.at[i])
        occ = [occ_in[i] for i in range(seg_count)]
        middle = start_in[...]
        for n in occ[:half]:
            middle = middle + jnp.where(n == 1, 1, 0) - jnp.where(n == 2, 1, 0)
        key_l = occ[3] * 64 + occ[2] * 16 + occ[1] * 4 + occ[0]
        key_l = jnp.where(lax.rem(middle + 2 * sec_count, sec_count) == sec, key_l, -1)
        key_r = occ[4] * 64 + occ[5] * 16 + occ[6] * 4 + occ[7]
        rows = lax.broadcasted_iota(jnp.int32, (256, 128), 0)
        for j in range(8):
            here = slice(j * 128, (j + 1) * 128)
            one_r[:, here] = rounded(jnp.where(rows == key_r[j:j + 1, :], 1.0, 0.0))
            one_l[:, here] = rounded(jnp.where(rows == key_l[j:j + 1, :], 1.0, 0.0))
        load.wait()

        def select(vectors, one_hot):
            return lax.dot_general(
                vectors, one_hot[...], (((0,), (0,)), ((), ())),
                preferred_element_type=jnp.float32,
            )

        for place in range(3):
            arrived(gath.at[place], gath_recv.at[place])
        for slot in range(4):
            arrived(z_in.at[slot], z_recv.at[slot])
        bond6 = [z_in[slot] for slot in range(4)]
        bond5 = []
        for place, turn in enumerate((0, 1, -1)):
            parts = [
                rounded(right_mul(bond6[(turn + CHARGE[n]) % 4], gath[place, n]))
                for n in range(4)
            ]
            bond5.append(jnp.concatenate(parts, axis=0))
        right = jnp.concatenate([rounded(part) for part in right_products(bond5)], axis=0)
        sel_r[...] = select(right, one_r)
        for n in range(4):
            arrived(left_in.at[n], l_recv.at[n])
        left = jnp.concatenate([left_in[n] for n in range(4)], axis=0)
        value = jnp.sum(select(left, one_l) * sel_r[...], axis=0, keepdims=True)
        for j in range(8):
            fin[sec, j:j + 1, :] = value[:, j * 128:(j + 1) * 128]
        count = seg_count * sec_count
        pl.semaphore_wait(barrier, count - 1)
        copies = ()

        def spread(seg_to, sec_to):
            return (
                send(
                    fin.at[sec], fin.at[sec], fin_send.at[len(copies)], fin_recv.at[sec],
                    seg_to, sec_to,
                ),
            )

        for j in range(sec_count):
            place = jnp.where(sec < sec_count // 2, sec_count - 1 - j, j)
            for i in range(seg_count):
                if i != hub:
                    copies += spread(i, place)
            if j > 0:
                copies += spread(hub, turned(j))
        finish(copies)

    for place in range(sec_count):
        @pl.when(jnp.logical_or(seg != hub, sec != place))
        def _():
            arrived(fin.at[place], fin_recv.at[place])

    out_ref[...] = (fin[0] + fin[1]) + (fin[2] + fin[3])


def tree_device(blocks, left_edge, right_edge, occupation, start_sector):
    seg_count = lax.axis_size("seg")
    sec_count = lax.axis_size("sec")
    hbm = pl.BlockSpec(memory_space=pl.ANY)
    dma = pltpu.SemaphoreType.DMA
    bf16, f32, i32 = jnp.bfloat16, jnp.float32, jnp.int32
    values = pl.pallas_call(
        functools.partial(tree_kernel, seg_count, sec_count),
        out_shape=jax.ShapeDtypeStruct((8, 128), f32),
        in_specs=[hbm] * 5,
        out_specs=pl.BlockSpec(memory_space=pltpu.VMEM),
        scratch_shapes=[
            pltpu.VMEM((4, 128, 128), bf16),
            pltpu.VMEM((4, 4, 128, 128), bf16),
            pltpu.VMEM((2, 128, 128), bf16),
            pltpu.VMEM((4, 16, 128), bf16),
            pltpu.VMEM((4, 16, 128), bf16),
            pltpu.VMEM((4, 16, 128), bf16),
            pltpu.VMEM((4, 64, 128), bf16),
            pltpu.VMEM((4, 64, 128), bf16),
            pltpu.VMEM((1, 128), bf16),
            pltpu.VMEM((4, 2, 16, 128), bf16),
            pltpu.VMEM((8, 8, 128), i32),
            pltpu.VMEM((8, 128), i32),
            pltpu.VMEM((256, 1024), bf16),
            pltpu.VMEM((256, 1024), bf16),
            pltpu.VMEM((128, 1024), f32),
            pltpu.VMEM((4, 8, 128), f32),
            dma, dma, dma, dma,
            dma((4,)),
            dma((3,)),
            dma((4,)),
            dma((6,)),
            dma((6,)),
            dma((4,)),
            dma((4,)),
            dma,
            dma((8,)),
            dma((seg_count * sec_count - 1,)),
            dma((4,)),
        ],
        compiler_params=pltpu.CompilerParams(
            collective_id=0, has_side_effects=True, vmem_limit_bytes=60 * 1024 * 1024
        ),
    )(
        blocks.reshape(4, 128, 128),
        left_edge,
        right_edge,
        occupation.reshape(8, 128),
        start_sector.reshape(8, 128),
    )
    return values.reshape(1024)


def fits_tree(mesh, blocks, occupation):
    seg_count, sec_count = mesh.shape["seg"], mesh.shape["sec"]
    return (
        seg_count == 8
        and sec_count == 4
        and blocks.shape == (8, 4, 4, 128, 128)
        and occupation.shape == (1024, 8)
    )


def padded_2(block, sides, width, periodic):
    for axis, dim in sides:
        count = lax.axis_size(axis)
        forward = [(i, i + 1) for i in range(count - 1)]
        if periodic:
            forward.append((count - 1, 0))
        backward = [(target, source) for source, target in forward]
        low = lax.ppermute(
            lax.slice_in_dim(block, block.shape[dim] - width, None, axis=dim), axis, forward
        )
        high = lax.ppermute(lax.slice_in_dim(block, 0, width, axis=dim), axis, backward)
        block = jnp.concatenate([low, block, high], axis=dim)
    return block


def state_masks(occ_site):
    levels = jnp.arange(4, dtype=jnp.int32)
    return (occ_site[:, None] == levels[None, :]).astype(jnp.float32)


def forward_send(vector, block_site, occ_masks):
    products = jnp.einsum("ka,nab->knb", vector, block_site, preferred_element_type=jnp.float32)
    terms = products * occ_masks[:, :, None]
    kept_term = (terms[:, 0] + terms[:, 3]).astype(jnp.bfloat16)
    upward = terms[:, 1].astype(jnp.bfloat16)
    downward = terms[:, 2].astype(jnp.bfloat16)
    return (kept_term, jnp.stack([downward, upward]))


def backward_send(vector, block_site, occ_masks):
    return (vector, jnp.stack([vector, vector]))


def forward_take(kept_term, padded, block_site, occ_masks):
    total = (
        kept_term.astype(jnp.float32)
        + padded[0].astype(jnp.float32)
        + padded[3].astype(jnp.float32)
    )
    return total.astype(jnp.bfloat16)


def backward_take(kept_term, padded, block_site, occ_masks):
    stacked = jnp.stack([kept_term, padded[3], padded[0], kept_term], axis=1)
    products = jnp.einsum("nab,knb->kna", block_site, stacked, preferred_element_type=jnp.float32)
    return jnp.sum(products * occ_masks[:, :, None], axis=1).astype(jnp.bfloat16)


def per_device(blocks, left_edge, right_edge, occupation, start_sector):
    seg_count = lax.axis_size("seg")
    half_count = seg_count // 2
    seg_index = lax.axis_index("seg")
    sec_index = lax.axis_index("sec")
    is_left = seg_index < half_count
    chain_depth = jnp.where(is_left, seg_index, seg_count - 1 - seg_index)
    is_first = chain_depth == 0
    meet_lower = seg_index == half_count - 1
    meet_upper = seg_index == half_count
    conf_count = occupation.shape[0]
    sites_here = occupation.shape[1]
    sector_width = blocks.shape[-1]
    block_count = 1
    columns = jnp.arange(sector_width, dtype=jnp.int32)
    lower_cols = (columns < sector_width // 2).astype(jnp.float32)
    upper_cols = 1.0 - lower_cols
    local_blocks = blocks[:, :, 0]
    left_row = left_edge[0]
    right_row = right_edge[0]
    batch_rows = conf_count // block_count

    def initial():
        zero_row = jnp.zeros_like(left_row)
        initial_left = jnp.where(
            (start_sector == sec_index)[:, None], left_row[None, :], zero_row[None, :]
        )
        initial_right = jnp.broadcast_to(right_row[None, :], (batch_rows, sector_width))
        return jnp.where(is_left, initial_left, initial_right)

    def run_sites(vector):
        position = jnp.where(is_left, 0, sites_here - 1)
        block_site = lax.dynamic_index_in_dim(local_blocks, position, 0, keepdims=False)
        occ_site = lax.dynamic_index_in_dim(occupation, position, 1, keepdims=False)
        occ_masks = state_masks(occ_site)
        kept_term, outgoing = lax.cond(
            is_left, forward_send, backward_send, vector, block_site, occ_masks
        )
        padded = padded_2(outgoing, (("sec", 0),), 1, True)
        vector = lax.cond(
            is_left, forward_take, backward_take, kept_term, padded, block_site, occ_masks
        )
        return vector

    section_count = half_count + block_count - 1

    def section(section_index, state_pair):
        incoming, partial_value = state_pair
        batch_index = section_index - chain_depth
        is_valid = (batch_index >= 0) & (batch_index < block_count)
        vector = jnp.where(is_first, initial(), incoming)
        vector = run_sites(vector)
        padded = padded_2(vector[None], (("seg", 0),), 1, False)
        received = jnp.where(is_left, padded[0], padded[2])
        own_vals = vector.astype(jnp.float32)
        lower_part = jnp.sum(own_vals * padded[2].astype(jnp.float32) * lower_cols[None, :], axis=1)
        upper_part = jnp.sum(own_vals * padded[0].astype(jnp.float32) * upper_cols[None, :], axis=1)
        product = jnp.where(meet_lower, lower_part, upper_part)
        previous = partial_value
        store_here = (meet_lower | meet_upper) & is_valid
        partial_value = jnp.where(store_here, product, previous)
        return (received, partial_value)

    start_state = (
        jnp.zeros((batch_rows, sector_width), jnp.bfloat16),
        jnp.zeros((conf_count,), jnp.float32),
    )
    final_state = lax.fori_loop(0, section_count, section, start_state)
    return lax.psum(final_state[1], ("seg", "sec"))


def solution(mesh):
    in_specs = (
        P("seg", None, "sec", None, None),
        P("sec", None),
        P("sec", None),
        P(None, "seg"),
        P(),
    )

    def run(blocks, left_edge, right_edge, occupation, start_sector):
        body = tree_device if fits_tree(mesh, blocks, occupation) else per_device
        return jax.shard_map(
            body, mesh=mesh, in_specs=in_specs, out_specs=P(), check_vma=False
        )(blocks, left_edge, right_edge, occupation, start_sector)

    return run
```

```python
import functools

import jax
import jax.numpy as jnp
from jax import lax
from jax.experimental import pallas as pl
from jax.experimental.pallas import tpu as pltpu
from jax.sharding import PartitionSpec as P

MESH = pl.DeviceIdType.MESH
CHARGE = (0, 1, -1, 0)
SITE2_PIECES = ((0, 0, 4), (1, 0, 1), (1, 2, 4), (2, 1, 3), (3, 0, 2), (3, 3, 4))


def tree_kernel(
    seg_count, sec_count,
    blocks_hbm, left_hbm, right_hbm, occ_hbm, start_hbm, fin,
    mats, gath, cross, x_in, z_in, y_out, left_out, left_in,
    edge, ends, occ_in, start_in, one_l, one_r, sel_r, part,
    load_sem, edge_sem, occ_sem, start_sem, ch_send, ch_recv, z_recv, gath_send, gath_recv,
    l_send, l_recv, occ_send, occ_recv, fin_send, fin_recv,
):
    seg = lax.axis_index("seg")
    sec = lax.axis_index("sec")
    up = lax.rem(sec + 1, sec_count)
    down = lax.rem(sec + sec_count - 1, sec_count)
    half = seg_count // 2
    last = seg_count - 1
    near = (sec, up, down)
    hub = half

    def turned(step):
        return lax.rem(sec + step, sec_count)

    load = pltpu.make_async_copy(blocks_hbm, mats, load_sem)
    barrier = pltpu.get_barrier_semaphore()

    def greet(seg_to, sec_to):
        pl.semaphore_signal(barrier, inc=1, device_id=(seg_to, sec_to), device_id_type=MESH)

    def greet_hubs():
        for step in range(sec_count):
            greet(hub, turned(step))

    def send(src, dst, send_sem, recv_sem, seg_to, sec_to):
        copy = pltpu.make_async_remote_copy(
            src_ref=src, dst_ref=dst, send_sem=send_sem, recv_sem=recv_sem,
            device_id=(seg_to, sec_to), device_id_type=MESH,
        )
        copy.start()
        return copy

    def arrived(dst, recv_sem):
        pltpu.make_async_remote_copy(
            src_ref=dst, dst_ref=dst, send_sem=ch_send.at[0], recv_sem=recv_sem,
            device_id=(seg, sec), device_id_type=MESH,
        ).wait_recv()

    def send_occ():
        return send(occ_hbm, occ_in.at[seg], occ_send, occ_recv.at[seg], hub, sec)

    rows16 = lax.broadcasted_iota(jnp.int32, (16, 128), 0)

    def pick(index, parts):
        total = parts[3]
        for n in (2, 1, 0):
            total = jnp.where(index == n, parts[n], total)
        return total

    def left_mul(x, block):
        return jnp.dot(x, block, preferred_element_type=jnp.float32)

    def right_mul(x, block):
        return lax.dot_general(
            x, block, (((1,), (1,)), ((), ())), preferred_element_type=jnp.float32
        )

    def rounded(x):
        return x.astype(jnp.bfloat16)

    def right_products(parts):
        return [right_mul(parts[place], mats[n]) for n, place in enumerate((0, 1, 2, 0))]

    def to_all(out, seg_to):
        copies = ()
        for step in range(sec_count):
            slot = (sec_count - step) % sec_count
            copies += (
                send(out, z_in.at[slot], ch_send.at[step], z_recv.at[slot], seg_to, turned(step)),
            )
        return copies

    def finish(copies):
        for copy in copies:
            copy.wait_send()

    def edge_load(ref):
        copy = pltpu.make_async_copy(ref, edge, edge_sem)
        copy.start()
        return copy

    def edge_rows():
        return rounded(jnp.broadcast_to(edge[...].astype(jnp.float32), (16, 128)))

    @pl.when(seg == 0)
    def _():
        edges = edge_load(left_hbm)
        load.start()
        greet_hubs()
        edges.wait()
        load.wait()
        x = edge_rows()
        for place, n in enumerate((0, 3, 1, 2)):
            y_out[place] = rounded(left_mul(x, mats[n]))
        pl.semaphore_wait(barrier, 4)
        copies = (
            send(y_out.at[2:3], x_in.at[2:3], ch_send.at[1], ch_recv.at[1], 1, up),
            send(y_out.at[3:4], x_in.at[3:4], ch_send.at[2], ch_recv.at[2], 1, down),
            send(y_out.at[0:2], x_in.at[0:2], ch_send.at[0], ch_recv.at[0], 1, sec),
        )
        occ = send_occ()
        finish(copies + (occ,))

    @pl.when(seg == 1)
    def _():
        for place in near:
            greet(0, place)
        greet_hubs()
        load.start()
        pl.semaphore_wait(barrier, 5)
        occ = send_occ()
        load.wait()
        arrived(x_in.at[0:2], ch_recv.at[0])
        arrived(x_in.at[2:3], ch_recv.at[1])
        arrived(x_in.at[3:4], ch_recv.at[2])
        parts = [x_in[place].astype(jnp.float32) for place in (0, 2, 3, 1)]
        x = rounded(pick(lax.rem(rows16, 4), parts))
        parts = [left_mul(x, mats[n]) for n in range(4)]
        y_out[0] = rounded(pick(lax.div(rows16, 4), parts))
        finish(to_all(y_out.at[0], 3) + (occ,))

    @pl.when(seg == 2)
    def _():
        greet_hubs()
        pl.semaphore_wait(barrier, 5)
        copies = ()
        for place, (turn, low, high) in enumerate(SITE2_PIECES):
            copies += (
                send(
                    blocks_hbm.at[low:high], gath.at[turn, low:high], gath_send.at[place],
                    gath_recv.at[place], 3, turned(sec_count - turn),
                ),
            )
        occ = send_occ()
        finish(copies + (occ,))

    @pl.when(seg == 3)
    def _():
        greet(3, up)
        greet(3, down)
        for step in range(sec_count):
            greet(2, turned(step))
        for step in range(sec_count):
            greet(1, turned(step))
        greet_hubs()
        load.start()
        pl.semaphore_wait(barrier, 3)
        copies = (
            send(blocks_hbm.at[1:2], cross.at[0:1], ch_send.at[0], ch_recv.at[0], 3, up),
            send(blocks_hbm.at[2:3], cross.at[1:2], ch_send.at[1], ch_recv.at[1], 3, down),
        )
        occ = send_occ()
        load.wait()
        arrived(cross.at[0:1], ch_recv.at[0])
        arrived(cross.at[1:2], ch_recv.at[1])
        for place, (turn, low, high) in enumerate(SITE2_PIECES):
            arrived(gath.at[turn, low:high], gath_recv.at[place])
        for slot in range(4):
            arrived(z_in.at[slot], z_recv.at[slot])
        heads = [z_in[slot].astype(jnp.float32) for slot in range(4)]
        block_rows = lax.div(rows16, 4)
        bond2 = [
            rounded(pick(block_rows, [heads[(turn - CHARGE[n]) % 4] for n in range(4)]))
            for turn in range(4)
        ]
        bond3 = {}
        for turn in (0, -1, 1):
            parts = []
            for n in range(4):
                source = (turn - CHARGE[n]) % 4
                parts.append(rounded(left_mul(bond2[source], gath[source, n])))
            bond3[turn] = jnp.concatenate(parts, axis=0)
        blocks3 = (mats[0], cross[0], cross[1], mats[3])
        for n in range(4):
            part = left_mul(bond3[-CHARGE[n]], blocks3[n])
            left_out[n] = rounded(part)
            copies += (
                send(left_out.at[n], left_in.at[n], l_send.at[n], l_recv.at[n], hub, sec),
            )
        finish(copies + (occ,))

    @pl.when(seg == last)
    def _():
        edges = edge_load(right_hbm)
        for step in range(1, sec_count):
            greet(last, turned(step))
        greet(last - 1, sec)
        greet_hubs()
        load.start()
        edges.wait()
        load.wait()
        own = edge_rows()
        kept = jnp.where(
            lax.rem(rows16, 4) == 0, right_mul(own, mats[0]), right_mul(own, mats[3])
        )
        ends[0, 0] = rounded(kept)
        ends[0, 1] = own
        pl.semaphore_wait(barrier, 7)
        copies = ()
        for step in (2, 1, 3):
            copies += (
                send(
                    ends.at[0], ends.at[sec_count - step], ch_send.at[step],
                    z_recv.at[sec_count - step], seg, turned(step),
                ),
            )
        for place, to in ((1, up), (0, down)):
            copies += (
                send(
                    blocks_hbm.at[1:3], gath.at[place, 1:3], gath_send.at[place],
                    gath_recv.at[place], seg, to,
                ),
            )
        occ = send_occ()
        for slot in range(1, 4):
            arrived(ends.at[slot], z_recv.at[slot])
        arrived(gath.at[2], gath_recv.at[2])
        for place in range(2):
            arrived(gath.at[place, 1:3], gath_recv.at[place])
        bond7 = []
        for turn, ones, twos in (
            (0, mats[1], mats[2]), (1, gath[0, 1], gath[0, 2]), (-1, gath[1, 1], gath[1, 2])
        ):
            kept = ends[turn % 4, 0].astype(jnp.float32)
            parts = [
                kept,
                right_mul(ends[(turn + 1) % 4, 1], ones),
                right_mul(ends[(turn - 1) % 4, 1], twos),
                kept,
            ]
            bond7.append(rounded(pick(lax.rem(rows16, 4), parts)))
        parts = [right_mul(bond7[place], gath[2, n]) for n, place in enumerate((0, 1, 2, 0))]
        y_out[0] = rounded(pick(lax.div(rows16, 4), parts))
        finish(copies)
        finish(to_all(y_out.at[0], hub) + (occ,))

    @pl.when(seg == 6)
    def _():
        greet_hubs()
        pl.semaphore_wait(barrier, 2)
        copy = send(blocks_hbm, gath.at[2], gath_send.at[0], gath_recv.at[2], last, sec)
        occ = send_occ()
        finish((copy, occ))

    @pl.when(seg == 5)
    def _():
        greet_hubs()
        pl.semaphore_wait(barrier, 3)
        copies = (
            send(blocks_hbm, gath.at[2], gath_send.at[1], gath_recv.at[2], hub, up),
            send(blocks_hbm, gath.at[1], gath_send.at[2], gath_recv.at[1], hub, down),
            send(blocks_hbm, gath.at[0], gath_send.at[0], gath_recv.at[0], hub, sec),
        )
        occ = send_occ()
        finish(copies + (occ,))

    @pl.when(seg == hub)
    def _():
        for step in (2, 1, 3, 0):
            greet(last, turned(step))
        greet(0, sec)
        for place in (up, down, sec):
            greet(hub + 1, place)
        for i in (1, 2, 3, last - 1):
            greet(i, sec)
        for step in range(1, sec_count):
            greet(hub, turned(step))
        load.start()
        own_occ = pltpu.make_async_copy(occ_hbm, occ_in.at[hub], occ_sem)
        own_occ.start()
        start = pltpu.make_async_copy(start_hbm, start_in, start_sem)
        start.start()
        own_occ.wait()
        start.wait()
        for i in range(seg_count):
            if i != hub:
                arrived(occ_in.at[i], occ_recv.at[i])
        occ = [occ_in[i] for i in range(seg_count)]
        middle = start_in[...]
        for n in occ[:half]:
            middle = middle + jnp.where(n == 1, 1, 0) - jnp.where(n == 2, 1, 0)
        key_l = occ[3] * 64 + occ[2] * 16 + occ[1] * 4 + occ[0]
        key_l = jnp.where(lax.rem(middle + 2 * sec_count, sec_count) == sec, key_l, -1)
        key_r = occ[4] * 64 + occ[5] * 16 + occ[6] * 4 + occ[7]
        rows = lax.broadcasted_iota(jnp.int32, (256, 128), 0)
        for j in range(8):
            here = slice(j * 128, (j + 1) * 128)
            one_r[:, here] = rounded(jnp.where(rows == key_r[j:j + 1, :], 1.0, 0.0))
            one_l[:, here] = rounded(jnp.where(rows == key_l[j:j + 1, :], 1.0, 0.0))
        load.wait()

        def select(vectors, one_hot):
            return lax.dot_general(
                vectors, one_hot[...], (((0,), (0,)), ((), ())),
                preferred_element_type=jnp.float32,
            )

        for place in range(3):
            arrived(gath.at[place], gath_recv.at[place])
        for slot in range(4):
            arrived(z_in.at[slot], z_recv.at[slot])
        bond6 = [z_in[slot] for slot in range(4)]
        bond5 = []
        for place, turn in enumerate((0, 1, -1)):
            parts = [
                rounded(right_mul(bond6[(turn + CHARGE[n]) % 4], gath[place, n]))
                for n in range(4)
            ]
            bond5.append(jnp.concatenate(parts, axis=0))
        right = jnp.concatenate([rounded(part) for part in right_products(bond5)], axis=0)
        sel_r[...] = select(right, one_r)
        for n in range(4):
            arrived(left_in.at[n], l_recv.at[n])
        left = jnp.concatenate([left_in[n] for n in range(4)], axis=0)
        value = jnp.sum(select(left, one_l) * sel_r[...], axis=0, keepdims=True)
        for j in range(8):
            part[j:j + 1, :] = value[:, j * 128:(j + 1) * 128]
        count = seg_count * sec_count
        pl.semaphore_wait(barrier, count - 1)
        copies = ()
        own = pltpu.make_async_copy(part, fin.at[sec], occ_sem)

        def spread(seg_to, sec_to):
            return (
                send(
                    part, fin.at[sec], fin_send.at[len(copies)], fin_recv.at[sec],
                    seg_to, sec_to,
                ),
            )

        for j in range(sec_count):
            place = jnp.where(sec < sec_count // 2, sec_count - 1 - j, j)
            for i in range(seg_count):
                if i != hub:
                    copies += spread(i, place)
            if j > 0:
                copies += spread(hub, turned(j))
        own.start()
        finish(copies)
        own.wait()

    for place in range(sec_count):
        @pl.when(jnp.logical_or(seg != hub, sec != place))
        def _():
            arrived(fin.at[place], fin_recv.at[place])


def tree_device(blocks, left_edge, right_edge, occupation, start_sector):
    seg_count = lax.axis_size("seg")
    sec_count = lax.axis_size("sec")
    hbm = pl.BlockSpec(memory_space=pl.ANY)
    dma = pltpu.SemaphoreType.DMA
    bf16, f32, i32 = jnp.bfloat16, jnp.float32, jnp.int32
    values = pl.pallas_call(
        functools.partial(tree_kernel, seg_count, sec_count),
        out_shape=jax.ShapeDtypeStruct((sec_count, 8, 128), f32),
        in_specs=[hbm] * 5,
        out_specs=hbm,
        scratch_shapes=[
            pltpu.VMEM((4, 128, 128), bf16),
            pltpu.VMEM((4, 4, 128, 128), bf16),
            pltpu.VMEM((2, 128, 128), bf16),
            pltpu.VMEM((4, 16, 128), bf16),
            pltpu.VMEM((4, 16, 128), bf16),
            pltpu.VMEM((4, 16, 128), bf16),
            pltpu.VMEM((4, 64, 128), bf16),
            pltpu.VMEM((4, 64, 128), bf16),
            pltpu.VMEM((1, 128), bf16),
            pltpu.VMEM((4, 2, 16, 128), bf16),
            pltpu.VMEM((8, 8, 128), i32),
            pltpu.VMEM((8, 128), i32),
            pltpu.VMEM((256, 1024), bf16),
            pltpu.VMEM((256, 1024), bf16),
            pltpu.VMEM((128, 1024), f32),
            pltpu.VMEM((8, 128), f32),
            dma, dma, dma, dma,
            dma((4,)),
            dma((3,)),
            dma((4,)),
            dma((6,)),
            dma((6,)),
            dma((4,)),
            dma((4,)),
            dma,
            dma((8,)),
            dma((seg_count * sec_count - 1,)),
            dma((4,)),
        ],
        compiler_params=pltpu.CompilerParams(
            collective_id=0, has_side_effects=True, vmem_limit_bytes=60 * 1024 * 1024
        ),
    )(
        blocks.reshape(4, 128, 128),
        left_edge,
        right_edge,
        occupation.reshape(8, 128),
        start_sector.reshape(8, 128),
    )
    return ((values[0] + values[1]) + (values[2] + values[3])).reshape(1024)


def fits_tree(mesh, blocks, occupation):
    seg_count, sec_count = mesh.shape["seg"], mesh.shape["sec"]
    return (
        seg_count == 8
        and sec_count == 4
        and blocks.shape == (8, 4, 4, 128, 128)
        and occupation.shape == (1024, 8)
    )


def padded_2(block, sides, width, periodic):
    for axis, dim in sides:
        count = lax.axis_size(axis)
        forward = [(i, i + 1) for i in range(count - 1)]
        if periodic:
            forward.append((count - 1, 0))
        backward = [(target, source) for source, target in forward]
        low = lax.ppermute(
            lax.slice_in_dim(block, block.shape[dim] - width, None, axis=dim), axis, forward
        )
        high = lax.ppermute(lax.slice_in_dim(block, 0, width, axis=dim), axis, backward)
        block = jnp.concatenate([low, block, high], axis=dim)
    return block


def state_masks(occ_site):
    levels = jnp.arange(4, dtype=jnp.int32)
    return (occ_site[:, None] == levels[None, :]).astype(jnp.float32)


def forward_send(vector, block_site, occ_masks):
    products = jnp.einsum("ka,nab->knb", vector, block_site, preferred_element_type=jnp.float32)
    terms = products * occ_masks[:, :, None]
    kept_term = (terms[:, 0] + terms[:, 3]).astype(jnp.bfloat16)
    upward = terms[:, 1].astype(jnp.bfloat16)
    downward = terms[:, 2].astype(jnp.bfloat16)
    return (kept_term, jnp.stack([downward, upward]))


def backward_send(vector, block_site, occ_masks):
    return (vector, jnp.stack([vector, vector]))


def forward_take(kept_term, padded, block_site, occ_masks):
    total = (
        kept_term.astype(jnp.float32)
        + padded[0].astype(jnp.float32)
        + padded[3].astype(jnp.float32)
    )
    return total.astype(jnp.bfloat16)


def backward_take(kept_term, padded, block_site, occ_masks):
    stacked = jnp.stack([kept_term, padded[3], padded[0], kept_term], axis=1)
    products = jnp.einsum("nab,knb->kna", block_site, stacked, preferred_element_type=jnp.float32)
    return jnp.sum(products * occ_masks[:, :, None], axis=1).astype(jnp.bfloat16)


def per_device(blocks, left_edge, right_edge, occupation, start_sector):
    seg_count = lax.axis_size("seg")
    half_count = seg_count // 2
    seg_index = lax.axis_index("seg")
    sec_index = lax.axis_index("sec")
    is_left = seg_index < half_count
    chain_depth = jnp.where(is_left, seg_index, seg_count - 1 - seg_index)
    is_first = chain_depth == 0
    meet_lower = seg_index == half_count - 1
    meet_upper = seg_index == half_count
    conf_count = occupation.shape[0]
    sites_here = occupation.shape[1]
    sector_width = blocks.shape[-1]
    block_count = 1
    columns = jnp.arange(sector_width, dtype=jnp.int32)
    lower_cols = (columns < sector_width // 2).astype(jnp.float32)
    upper_cols = 1.0 - lower_cols
    local_blocks = blocks[:, :, 0]
    left_row = left_edge[0]
    right_row = right_edge[0]
    batch_rows = conf_count // block_count

    def initial():
        zero_row = jnp.zeros_like(left_row)
        initial_left = jnp.where(
            (start_sector == sec_index)[:, None], left_row[None, :], zero_row[None, :]
        )
        initial_right = jnp.broadcast_to(right_row[None, :], (batch_rows, sector_width))
        return jnp.where(is_left, initial_left, initial_right)

    def run_sites(vector):
        position = jnp.where(is_left, 0, sites_here - 1)
        block_site = lax.dynamic_index_in_dim(local_blocks, position, 0, keepdims=False)
        occ_site = lax.dynamic_index_in_dim(occupation, position, 1, keepdims=False)
        occ_masks = state_masks(occ_site)
        kept_term, outgoing = lax.cond(
            is_left, forward_send, backward_send, vector, block_site, occ_masks
        )
        padded = padded_2(outgoing, (("sec", 0),), 1, True)
        vector = lax.cond(
            is_left, forward_take, backward_take, kept_term, padded, block_site, occ_masks
        )
        return vector

    section_count = half_count + block_count - 1

    def section(section_index, state_pair):
        incoming, partial_value = state_pair
        batch_index = section_index - chain_depth
        is_valid = (batch_index >= 0) & (batch_index < block_count)
        vector = jnp.where(is_first, initial(), incoming)
        vector = run_sites(vector)
        padded = padded_2(vector[None], (("seg", 0),), 1, False)
        received = jnp.where(is_left, padded[0], padded[2])
        own_vals = vector.astype(jnp.float32)
        lower_part = jnp.sum(own_vals * padded[2].astype(jnp.float32) * lower_cols[None, :], axis=1)
        upper_part = jnp.sum(own_vals * padded[0].astype(jnp.float32) * upper_cols[None, :], axis=1)
        product = jnp.where(meet_lower, lower_part, upper_part)
        previous = partial_value
        store_here = (meet_lower | meet_upper) & is_valid
        partial_value = jnp.where(store_here, product, previous)
        return (received, partial_value)

    start_state = (
        jnp.zeros((batch_rows, sector_width), jnp.bfloat16),
        jnp.zeros((conf_count,), jnp.float32),
    )
    final_state = lax.fori_loop(0, section_count, section, start_state)
    return lax.psum(final_state[1], ("seg", "sec"))


def solution(mesh):
    in_specs = (
        P("seg", None, "sec", None, None),
        P("sec", None),
        P("sec", None),
        P(None, "seg"),
        P(),
    )

    def run(blocks, left_edge, right_edge, occupation, start_sector):
        body = tree_device if fits_tree(mesh, blocks, occupation) else per_device
        return jax.shard_map(
            body, mesh=mesh, in_specs=in_specs, out_specs=P(), check_vma=False
        )(blocks, left_edge, right_edge, occupation, start_sector)

    return run
```

```python
import functools

import jax
import jax.numpy as jnp
from jax import lax
from jax.experimental import pallas as pl
from jax.experimental.pallas import tpu as pltpu
from jax.sharding import PartitionSpec as P

MESH = pl.DeviceIdType.MESH
CHARGE = (0, 1, -1, 0)
SITE2_PIECES = ((1, 0, 1), (1, 2, 4), (2, 1, 3), (3, 0, 2), (3, 3, 4))


def tree_kernel(
    seg_count, sec_count,
    blocks_hbm, left_hbm, right_hbm, occ_hbm, start_hbm, fin,
    mats, gath, cross, x_in, z_in, y_out, left_out, left_in,
    edge, ends, theirs, occ_in, start_in, one_l, one_r, sel_r, part,
    load_sem, edge_sem, occ_sem, start_sem, ch_send, ch_recv, z_recv, gath_send, gath_recv,
    l_send, l_recv, occ_send, occ_recv, fin_send, fin_recv,
):
    seg = lax.axis_index("seg")
    sec = lax.axis_index("sec")
    up = lax.rem(sec + 1, sec_count)
    down = lax.rem(sec + sec_count - 1, sec_count)
    half = seg_count // 2
    last = seg_count - 1
    near = (sec, up, down)
    hub = half + 1

    def turned(step):
        return lax.rem(sec + step, sec_count)

    load = pltpu.make_async_copy(blocks_hbm, mats, load_sem)
    barrier = pltpu.get_barrier_semaphore()

    def greet(seg_to, sec_to):
        pl.semaphore_signal(barrier, inc=1, device_id=(seg_to, sec_to), device_id_type=MESH)

    def greet_hubs():
        for step in range(sec_count):
            greet(hub, turned(step))

    def send(src, dst, send_sem, recv_sem, seg_to, sec_to):
        copy = pltpu.make_async_remote_copy(
            src_ref=src, dst_ref=dst, send_sem=send_sem, recv_sem=recv_sem,
            device_id=(seg_to, sec_to), device_id_type=MESH,
        )
        copy.start()
        return copy

    def arrived(dst, recv_sem):
        pltpu.make_async_remote_copy(
            src_ref=dst, dst_ref=dst, send_sem=ch_send.at[0], recv_sem=recv_sem,
            device_id=(seg, sec), device_id_type=MESH,
        ).wait_recv()

    def send_occ():
        return send(occ_hbm, occ_in.at[seg], occ_send, occ_recv.at[seg], hub, sec)

    rows16 = lax.broadcasted_iota(jnp.int32, (16, 128), 0)

    def pick(index, parts):
        total = parts[3]
        for n in (2, 1, 0):
            total = jnp.where(index == n, parts[n], total)
        return total

    def left_mul(x, block):
        return jnp.dot(x, block, preferred_element_type=jnp.float32)

    def right_mul(x, block):
        return lax.dot_general(
            x, block, (((1,), (1,)), ((), ())), preferred_element_type=jnp.float32
        )

    def rounded(x):
        return x.astype(jnp.bfloat16)

    def to_all(out, seg_to):
        copies = ()
        for step in range(sec_count):
            slot = (sec_count - step) % sec_count
            copies += (
                send(out, z_in.at[slot], ch_send.at[step], z_recv.at[slot], seg_to, turned(step)),
            )
        return copies

    def finish(copies):
        for copy in copies:
            copy.wait_send()

    def edge_load(ref):
        copy = pltpu.make_async_copy(ref, edge, edge_sem)
        copy.start()
        return copy

    def edge_rows():
        return rounded(jnp.broadcast_to(edge[...].astype(jnp.float32), (16, 128)))

    @pl.when(seg == 0)
    def _():
        edges = edge_load(left_hbm)
        load.start()
        greet_hubs()
        edges.wait()
        load.wait()
        x = edge_rows()
        for place, n in enumerate((0, 3, 1, 2)):
            y_out[place] = rounded(left_mul(x, mats[n]))
        pl.semaphore_wait(barrier, 4)
        copies = (
            send(y_out.at[2:3], x_in.at[2:3], ch_send.at[1], ch_recv.at[1], 1, up),
            send(y_out.at[3:4], x_in.at[3:4], ch_send.at[2], ch_recv.at[2], 1, down),
            send(y_out.at[0:2], x_in.at[0:2], ch_send.at[0], ch_recv.at[0], 1, sec),
        )
        occ = send_occ()
        finish(copies + (occ,))

    @pl.when(seg == 1)
    def _():
        for place in near:
            greet(0, place)
        greet_hubs()
        load.start()
        pl.semaphore_wait(barrier, 5)
        occ = send_occ()
        load.wait()
        arrived(x_in.at[0:2], ch_recv.at[0])
        arrived(x_in.at[2:3], ch_recv.at[1])
        arrived(x_in.at[3:4], ch_recv.at[2])
        parts = [x_in[place].astype(jnp.float32) for place in (0, 2, 3, 1)]
        x = rounded(pick(lax.rem(rows16, 4), parts))
        parts = [left_mul(x, mats[n]) for n in range(4)]
        y_out[0] = rounded(pick(lax.div(rows16, 4), parts))
        finish(to_all(y_out.at[0], 2) + (occ,))

    @pl.when(seg == 3)
    def _():
        greet_hubs()
        pl.semaphore_wait(barrier, 4)
        copies = ()
        for n, to in ((1, up), (2, down), (0, sec), (3, sec)):
            copies += (
                send(
                    blocks_hbm.at[n:n + 1], cross.at[n:n + 1], l_send.at[n], l_recv.at[n], 2, to
                ),
            )
        occ = send_occ()
        finish(copies + (occ,))

    @pl.when(seg == 2)
    def _():
        for step in range(1, sec_count):
            greet(2, turned(step))
        for place in near:
            greet(3, place)
        for step in range(sec_count):
            greet(1, turned(step))
        greet_hubs()
        load.start()
        pl.semaphore_wait(barrier, 4)
        copies = ()
        for place, (turn, low, high) in enumerate(SITE2_PIECES):
            copies += (
                send(
                    blocks_hbm.at[low:high], gath.at[turn, low:high], gath_send.at[place],
                    gath_recv.at[place], 2, turned(sec_count - turn),
                ),
            )
        occ = send_occ()
        load.wait()
        for n in range(4):
            arrived(cross.at[n:n + 1], l_recv.at[n])
        for place, (turn, low, high) in enumerate(SITE2_PIECES):
            arrived(gath.at[turn, low:high], gath_recv.at[place])
        for slot in range(4):
            arrived(z_in.at[slot], z_recv.at[slot])
        heads = [z_in[slot].astype(jnp.float32) for slot in range(4)]
        block_rows = lax.div(rows16, 4)
        bond2 = [
            rounded(pick(block_rows, [heads[(turn - CHARGE[n]) % 4] for n in range(4)]))
            for turn in range(4)
        ]
        bond3 = {}
        for turn in (0, -1, 1):
            parts = []
            for n in range(4):
                source = (turn - CHARGE[n]) % 4
                parts.append(rounded(left_mul(bond2[source], mats[n] if source == 0 else gath[source, n])))
            bond3[turn] = jnp.concatenate(parts, axis=0)
        for n in range(4):
            part = left_mul(bond3[-CHARGE[n]], cross[n])
            left_out[n] = rounded(part)
            copies += (
                send(left_out.at[n], left_in.at[n], l_send.at[n], l_recv.at[n], hub, sec),
            )
        finish(copies + (occ,))

    @pl.when(seg == last)
    def _():
        edges = edge_load(right_hbm)
        greet_hubs()
        load.start()
        edges.wait()
        load.wait()
        own = edge_rows()
        kept = jnp.where(
            lax.rem(rows16, 4) == 0, right_mul(own, mats[0]), right_mul(own, mats[3])
        )
        ends[0, 0] = rounded(kept)
        ends[0, 1] = own
        pl.semaphore_wait(barrier, 5)
        copies = ()
        for step in (2, 1, 3, 0):
            slot = (sec_count - step) % sec_count
            copies += (
                send(
                    ends.at[0], theirs.at[slot], ch_send.at[step], z_recv.at[slot],
                    last - 1, turned(step),
                ),
            )
        for place, to in ((1, up), (0, down), (2, sec)):
            copies += (
                send(
                    blocks_hbm.at[1:3], gath.at[place, 1:3], gath_send.at[place],
                    gath_recv.at[place], last - 1, to,
                ),
            )
        occ = send_occ()
        finish(copies + (occ,))

    @pl.when(seg == last - 1)
    def _():
        for step in (2, 1, 3, 0):
            greet(last, turned(step))
        greet_hubs()
        load.start()
        pl.semaphore_wait(barrier, 4)
        occ = send_occ()
        load.wait()
        for slot in range(4):
            arrived(theirs.at[slot], z_recv.at[slot])
        for place in range(3):
            arrived(gath.at[place, 1:3], gath_recv.at[place])
        bond7 = []
        for turn, ones, twos in (
            (0, gath[2, 1], gath[2, 2]), (1, gath[0, 1], gath[0, 2]), (-1, gath[1, 1], gath[1, 2])
        ):
            kept = theirs[turn % 4, 0].astype(jnp.float32)
            parts = [
                kept,
                right_mul(theirs[(turn + 1) % 4, 1], ones),
                right_mul(theirs[(turn - 1) % 4, 1], twos),
                kept,
            ]
            bond7.append(rounded(pick(lax.rem(rows16, 4), parts)))
        parts = [right_mul(bond7[place], mats[n]) for n, place in enumerate((0, 1, 2, 0))]
        y_out[0] = rounded(pick(lax.div(rows16, 4), parts))
        finish(to_all(y_out.at[0], hub) + (occ,))

    @pl.when(seg == half)
    def _():
        greet_hubs()
        pl.semaphore_wait(barrier, 1)
        copy = send(blocks_hbm, gath.at[0], gath_send.at[0], gath_recv.at[0], hub, sec)
        occ = send_occ()
        finish((copy, occ))

    @pl.when(seg == hub)
    def _():
        for i in (last, 0):
            greet(i, sec)
        for step in range(1, sec_count):
            greet(hub, turned(step))
        for step in range(sec_count):
            greet(last - 1, turned(step))
        for i in (1, 2, 3, half):
            greet(i, sec)
        load.start()
        own_occ = pltpu.make_async_copy(occ_hbm, occ_in.at[hub], occ_sem)
        own_occ.start()
        start = pltpu.make_async_copy(start_hbm, start_in, start_sem)
        start.start()
        count = seg_count * sec_count
        pl.semaphore_wait(barrier, count - 1)
        given = (
            send(blocks_hbm, gath.at[2], gath_send.at[1], gath_recv.at[2], hub, up),
            send(blocks_hbm, gath.at[1], gath_send.at[2], gath_recv.at[1], hub, down),
        )
        own_occ.wait()
        start.wait()
        for i in range(seg_count):
            if i != hub:
                arrived(occ_in.at[i], occ_recv.at[i])
        occ = [occ_in[i] for i in range(seg_count)]
        middle = start_in[...]
        for n in occ[:half]:
            middle = middle + jnp.where(n == 1, 1, 0) - jnp.where(n == 2, 1, 0)
        key_l = occ[3] * 64 + occ[2] * 16 + occ[1] * 4 + occ[0]
        key_l = jnp.where(lax.rem(middle + 2 * sec_count, sec_count) == sec, key_l, -1)
        key_r = occ[4] * 64 + occ[5] * 16 + occ[6] * 4 + occ[7]
        rows = lax.broadcasted_iota(jnp.int32, (256, 128), 0)
        for j in range(8):
            here = slice(j * 128, (j + 1) * 128)
            one_r[:, here] = rounded(jnp.where(rows == key_r[j:j + 1, :], 1.0, 0.0))
            one_l[:, here] = rounded(jnp.where(rows == key_l[j:j + 1, :], 1.0, 0.0))
        load.wait()

        def select(vectors, one_hot):
            return lax.dot_general(
                vectors, one_hot[...], (((0,), (0,)), ((), ())),
                preferred_element_type=jnp.float32,
            )

        for place in range(3):
            arrived(gath.at[place], gath_recv.at[place])
        for slot in range(4):
            arrived(z_in.at[slot], z_recv.at[slot])
        bond6 = [z_in[slot] for slot in range(4)]
        bond5 = []
        for place, turn in enumerate((0, 1, -1)):
            parts = [
                rounded(right_mul(bond6[(turn + CHARGE[n]) % 4], gath[place, n] if place else mats[n]))
                for n in range(4)
            ]
            bond5.append(jnp.concatenate(parts, axis=0))
        site4 = [right_mul(bond5[place], gath[0, n]) for n, place in enumerate((0, 1, 2, 0))]
        right = jnp.concatenate([rounded(part) for part in site4], axis=0)
        sel_r[...] = select(right, one_r)
        for n in range(4):
            arrived(left_in.at[n], l_recv.at[n])
        left = jnp.concatenate([left_in[n] for n in range(4)], axis=0)
        value = jnp.sum(select(left, one_l) * sel_r[...], axis=0, keepdims=True)
        for j in range(8):
            part[j:j + 1, :] = value[:, j * 128:(j + 1) * 128]
        copies = ()
        own = pltpu.make_async_copy(part, fin.at[sec], occ_sem)

        def spread(seg_to, sec_to):
            return (
                send(
                    part, fin.at[sec], fin_send.at[len(copies)], fin_recv.at[sec],
                    seg_to, sec_to,
                ),
            )

        for j in range(sec_count):
            place = jnp.where(sec < sec_count // 2, sec_count - 1 - j, j)
            for i in range(seg_count):
                if i != hub:
                    copies += spread(i, place)
            if j > 0:
                copies += spread(hub, turned(j))
        own.start()
        finish(copies + given)
        own.wait()

    for place in range(sec_count):
        @pl.when(jnp.logical_or(seg != hub, sec != place))
        def _():
            arrived(fin.at[place], fin_recv.at[place])


def tree_device(blocks, left_edge, right_edge, occupation, start_sector):
    seg_count = lax.axis_size("seg")
    sec_count = lax.axis_size("sec")
    hbm = pl.BlockSpec(memory_space=pl.ANY)
    dma = pltpu.SemaphoreType.DMA
    bf16, f32, i32 = jnp.bfloat16, jnp.float32, jnp.int32
    values = pl.pallas_call(
        functools.partial(tree_kernel, seg_count, sec_count),
        out_shape=jax.ShapeDtypeStruct((sec_count, 8, 128), f32),
        in_specs=[hbm] * 5,
        out_specs=hbm,
        scratch_shapes=[
            pltpu.VMEM((4, 128, 128), bf16),
            pltpu.VMEM((4, 4, 128, 128), bf16),
            pltpu.VMEM((4, 128, 128), bf16),
            pltpu.VMEM((4, 16, 128), bf16),
            pltpu.VMEM((4, 16, 128), bf16),
            pltpu.VMEM((4, 16, 128), bf16),
            pltpu.VMEM((4, 64, 128), bf16),
            pltpu.VMEM((4, 64, 128), bf16),
            pltpu.VMEM((1, 128), bf16),
            pltpu.VMEM((1, 2, 16, 128), bf16),
            pltpu.VMEM((4, 2, 16, 128), bf16),
            pltpu.VMEM((8, 8, 128), i32),
            pltpu.VMEM((8, 128), i32),
            pltpu.VMEM((256, 1024), bf16),
            pltpu.VMEM((256, 1024), bf16),
            pltpu.VMEM((128, 1024), f32),
            pltpu.VMEM((8, 128), f32),
            dma, dma, dma, dma,
            dma((4,)),
            dma((3,)),
            dma((4,)),
            dma((6,)),
            dma((6,)),
            dma((4,)),
            dma((4,)),
            dma,
            dma((8,)),
            dma((seg_count * sec_count - 1,)),
            dma((4,)),
        ],
        compiler_params=pltpu.CompilerParams(
            collective_id=0, has_side_effects=True, vmem_limit_bytes=60 * 1024 * 1024
        ),
    )(
        blocks.reshape(4, 128, 128),
        left_edge,
        right_edge,
        occupation.reshape(8, 128),
        start_sector.reshape(8, 128),
    )
    return ((values[0] + values[1]) + (values[2] + values[3])).reshape(1024)


def fits_tree(mesh, blocks, occupation):
    seg_count, sec_count = mesh.shape["seg"], mesh.shape["sec"]
    return (
        seg_count == 8
        and sec_count == 4
        and blocks.shape == (8, 4, 4, 128, 128)
        and occupation.shape == (1024, 8)
    )


def padded_2(block, sides, width, periodic):
    for axis, dim in sides:
        count = lax.axis_size(axis)
        forward = [(i, i + 1) for i in range(count - 1)]
        if periodic:
            forward.append((count - 1, 0))
        backward = [(target, source) for source, target in forward]
        low = lax.ppermute(
            lax.slice_in_dim(block, block.shape[dim] - width, None, axis=dim), axis, forward
        )
        high = lax.ppermute(lax.slice_in_dim(block, 0, width, axis=dim), axis, backward)
        block = jnp.concatenate([low, block, high], axis=dim)
    return block


def state_masks(occ_site):
    levels = jnp.arange(4, dtype=jnp.int32)
    return (occ_site[:, None] == levels[None, :]).astype(jnp.float32)


def forward_send(vector, block_site, occ_masks):
    products = jnp.einsum("ka,nab->knb", vector, block_site, preferred_element_type=jnp.float32)
    terms = products * occ_masks[:, :, None]
    kept_term = (terms[:, 0] + terms[:, 3]).astype(jnp.bfloat16)
    upward = terms[:, 1].astype(jnp.bfloat16)
    downward = terms[:, 2].astype(jnp.bfloat16)
    return (kept_term, jnp.stack([downward, upward]))


def backward_send(vector, block_site, occ_masks):
    return (vector, jnp.stack([vector, vector]))


def forward_take(kept_term, padded, block_site, occ_masks):
    total = (
        kept_term.astype(jnp.float32)
        + padded[0].astype(jnp.float32)
        + padded[3].astype(jnp.float32)
    )
    return total.astype(jnp.bfloat16)


def backward_take(kept_term, padded, block_site, occ_masks):
    stacked = jnp.stack([kept_term, padded[3], padded[0], kept_term], axis=1)
    products = jnp.einsum("nab,knb->kna", block_site, stacked, preferred_element_type=jnp.float32)
    return jnp.sum(products * occ_masks[:, :, None], axis=1).astype(jnp.bfloat16)


def per_device(blocks, left_edge, right_edge, occupation, start_sector):
    seg_count = lax.axis_size("seg")
    half_count = seg_count // 2
    seg_index = lax.axis_index("seg")
    sec_index = lax.axis_index("sec")
    is_left = seg_index < half_count
    chain_depth = jnp.where(is_left, seg_index, seg_count - 1 - seg_index)
    is_first = chain_depth == 0
    meet_lower = seg_index == half_count - 1
    meet_upper = seg_index == half_count
    conf_count = occupation.shape[0]
    sites_here = occupation.shape[1]
    sector_width = blocks.shape[-1]
    block_count = 1
    columns = jnp.arange(sector_width, dtype=jnp.int32)
    lower_cols = (columns < sector_width // 2).astype(jnp.float32)
    upper_cols = 1.0 - lower_cols
    local_blocks = blocks[:, :, 0]
    left_row = left_edge[0]
    right_row = right_edge[0]
    batch_rows = conf_count // block_count

    def initial():
        zero_row = jnp.zeros_like(left_row)
        initial_left = jnp.where(
            (start_sector == sec_index)[:, None], left_row[None, :], zero_row[None, :]
        )
        initial_right = jnp.broadcast_to(right_row[None, :], (batch_rows, sector_width))
        return jnp.where(is_left, initial_left, initial_right)

    def run_sites(vector):
        position = jnp.where(is_left, 0, sites_here - 1)
        block_site = lax.dynamic_index_in_dim(local_blocks, position, 0, keepdims=False)
        occ_site = lax.dynamic_index_in_dim(occupation, position, 1, keepdims=False)
        occ_masks = state_masks(occ_site)
        kept_term, outgoing = lax.cond(
            is_left, forward_send, backward_send, vector, block_site, occ_masks
        )
        padded = padded_2(outgoing, (("sec", 0),), 1, True)
        vector = lax.cond(
            is_left, forward_take, backward_take, kept_term, padded, block_site, occ_masks
        )
        return vector

    section_count = half_count + block_count - 1

    def section(section_index, state_pair):
        incoming, partial_value = state_pair
        batch_index = section_index - chain_depth
        is_valid = (batch_index >= 0) & (batch_index < block_count)
        vector = jnp.where(is_first, initial(), incoming)
        vector = run_sites(vector)
        padded = padded_2(vector[None], (("seg", 0),), 1, False)
        received = jnp.where(is_left, padded[0], padded[2])
        own_vals = vector.astype(jnp.float32)
        lower_part = jnp.sum(own_vals * padded[2].astype(jnp.float32) * lower_cols[None, :], axis=1)
        upper_part = jnp.sum(own_vals * padded[0].astype(jnp.float32) * upper_cols[None, :], axis=1)
        product = jnp.where(meet_lower, lower_part, upper_part)
        previous = partial_value
        store_here = (meet_lower | meet_upper) & is_valid
        partial_value = jnp.where(store_here, product, previous)
        return (received, partial_value)

    start_state = (
        jnp.zeros((batch_rows, sector_width), jnp.bfloat16),
        jnp.zeros((conf_count,), jnp.float32),
    )
    final_state = lax.fori_loop(0, section_count, section, start_state)
    return lax.psum(final_state[1], ("seg", "sec"))


def solution(mesh):
    in_specs = (
        P("seg", None, "sec", None, None),
        P("sec", None),
        P("sec", None),
        P(None, "seg"),
        P(),
    )

    def run(blocks, left_edge, right_edge, occupation, start_sector):
        body = tree_device if fits_tree(mesh, blocks, occupation) else per_device
        return jax.shard_map(
            body, mesh=mesh, in_specs=in_specs, out_specs=P(), check_vma=False
        )(blocks, left_edge, right_edge, occupation, start_sector)

    return run
```

```python
import functools

import jax
import jax.numpy as jnp
from jax import lax
from jax.experimental import pallas as pl
from jax.experimental.pallas import tpu as pltpu
from jax.sharding import PartitionSpec as P

MESH = pl.DeviceIdType.MESH
CHARGE = (0, 1, -1, 0)
SITE2_PIECES = ((2, 1, 3), (1, 0, 1), (1, 2, 4), (3, 0, 2), (3, 3, 4), (0, 0, 4))


def tree_kernel(
    seg_count, sec_count,
    blocks_hbm, left_hbm, right_hbm, occ_hbm, start_hbm, fin,
    mats, gath, cross, x_in, z_in, y_out, left_out, left_in,
    edge, ends, occ_in, start_in, one_l, one_r, sel_r, part,
    load_sem, edge_sem, occ_sem, start_sem, ch_send, ch_recv, z_recv, gath_send, gath_recv,
    l_send, l_recv, occ_send, occ_recv, fin_send, fin_recv,
):
    seg = lax.axis_index("seg")
    sec = lax.axis_index("sec")
    up = lax.rem(sec + 1, sec_count)
    down = lax.rem(sec + sec_count - 1, sec_count)
    half = seg_count // 2
    last = seg_count - 1
    near = (sec, up, down)
    hub = half

    def turned(step):
        return lax.rem(sec + step, sec_count)

    load = pltpu.make_async_copy(blocks_hbm, mats, load_sem)
    barrier = pltpu.get_barrier_semaphore()

    def greet(seg_to, sec_to):
        pl.semaphore_signal(barrier, inc=1, device_id=(seg_to, sec_to), device_id_type=MESH)

    def greet_hubs():
        for step in range(sec_count):
            greet(hub, turned(step))

    def send(src, dst, send_sem, recv_sem, seg_to, sec_to):
        copy = pltpu.make_async_remote_copy(
            src_ref=src, dst_ref=dst, send_sem=send_sem, recv_sem=recv_sem,
            device_id=(seg_to, sec_to), device_id_type=MESH,
        )
        copy.start()
        return copy

    def arrived(dst, recv_sem):
        pltpu.make_async_remote_copy(
            src_ref=dst, dst_ref=dst, send_sem=ch_send.at[0], recv_sem=recv_sem,
            device_id=(seg, sec), device_id_type=MESH,
        ).wait_recv()

    def send_occ():
        return send(occ_hbm, occ_in.at[seg], occ_send, occ_recv.at[seg], hub, sec)

    rows16 = lax.broadcasted_iota(jnp.int32, (16, 128), 0)

    def pick(index, parts):
        total = parts[3]
        for n in (2, 1, 0):
            total = jnp.where(index == n, parts[n], total)
        return total

    def left_mul(x, block):
        return jnp.dot(x, block, preferred_element_type=jnp.float32)

    def right_mul(x, block):
        return lax.dot_general(
            x, block, (((1,), (1,)), ((), ())), preferred_element_type=jnp.float32
        )

    def rounded(x):
        return x.astype(jnp.bfloat16)

    def right_products(parts):
        return [right_mul(parts[place], mats[n]) for n, place in enumerate((0, 1, 2, 0))]

    def to_all(out, seg_to):
        copies = ()
        for step in (1, 3, 2, 0):
            slot = (sec_count - step) % sec_count
            copies += (
                send(out, z_in.at[slot], ch_send.at[step], z_recv.at[slot], seg_to, turned(step)),
            )
        return copies

    def finish(copies):
        for copy in copies:
            copy.wait_send()

    def edge_load(ref):
        copy = pltpu.make_async_copy(ref, edge, edge_sem)
        copy.start()
        return copy

    def edge_rows():
        return rounded(jnp.broadcast_to(edge[...].astype(jnp.float32), (16, 128)))

    @pl.when(seg == 0)
    def _():
        edges = edge_load(left_hbm)
        load.start()
        greet_hubs()
        edges.wait()
        load.wait()
        x = edge_rows()
        for place, n in enumerate((0, 3, 1, 2)):
            y_out[place] = rounded(left_mul(x, mats[n]))
        pl.semaphore_wait(barrier, 4)
        copies = (
            send(y_out.at[2:3], x_in.at[2:3], ch_send.at[1], ch_recv.at[1], 1, up),
            send(y_out.at[3:4], x_in.at[3:4], ch_send.at[2], ch_recv.at[2], 1, down),
            send(y_out.at[0:2], x_in.at[0:2], ch_send.at[0], ch_recv.at[0], 1, sec),
        )
        occ = send_occ()
        finish(copies + (occ,))

    @pl.when(seg == 1)
    def _():
        for place in near:
            greet(0, place)
        greet_hubs()
        load.start()
        pl.semaphore_wait(barrier, 5)
        occ = send_occ()
        load.wait()
        arrived(x_in.at[0:2], ch_recv.at[0])
        arrived(x_in.at[2:3], ch_recv.at[1])
        arrived(x_in.at[3:4], ch_recv.at[2])
        parts = [x_in[place].astype(jnp.float32) for place in (0, 2, 3, 1)]
        x = rounded(pick(lax.rem(rows16, 4), parts))
        parts = [left_mul(x, mats[n]) for n in range(4)]
        y_out[0] = rounded(pick(lax.div(rows16, 4), parts))
        finish(to_all(y_out.at[0], 3) + (occ,))

    @pl.when(seg == 2)
    def _():
        greet_hubs()
        pl.semaphore_wait(barrier, 5)
        copies = ()
        for place, (turn, low, high) in enumerate(SITE2_PIECES):
            copies += (
                send(
                    blocks_hbm.at[low:high], gath.at[turn, low:high], gath_send.at[place],
                    gath_recv.at[place], 3, turned(sec_count - turn),
                ),
            )
        occ = send_occ()
        finish(copies + (occ,))

    @pl.when(seg == 3)
    def _():
        greet(3, up)
        greet(3, down)
        for step in range(sec_count):
            greet(2, turned(step))
        for step in range(sec_count):
            greet(1, turned(step))
        greet_hubs()
        load.start()
        pl.semaphore_wait(barrier, 3)
        copies = (
            send(blocks_hbm.at[1:2], cross.at[0:1], ch_send.at[0], ch_recv.at[0], 3, up),
            send(blocks_hbm.at[2:3], cross.at[1:2], ch_send.at[1], ch_recv.at[1], 3, down),
        )
        occ = send_occ()
        load.wait()
        arrived(cross.at[0:1], ch_recv.at[0])
        arrived(cross.at[1:2], ch_recv.at[1])
        for place, (turn, low, high) in enumerate(SITE2_PIECES):
            arrived(gath.at[turn, low:high], gath_recv.at[place])
        for slot in range(4):
            arrived(z_in.at[slot], z_recv.at[slot])
        heads = [z_in[slot].astype(jnp.float32) for slot in range(4)]
        block_rows = lax.div(rows16, 4)
        bond2 = [
            rounded(pick(block_rows, [heads[(turn - CHARGE[n]) % 4] for n in range(4)]))
            for turn in range(4)
        ]
        bond3 = {}
        for turn in (0, -1, 1):
            parts = []
            for n in range(4):
                source = (turn - CHARGE[n]) % 4
                parts.append(rounded(left_mul(bond2[source], gath[source, n])))
            bond3[turn] = jnp.concatenate(parts, axis=0)
        blocks3 = (mats[0], cross[0], cross[1], mats[3])
        for n in range(4):
            part = left_mul(bond3[-CHARGE[n]], blocks3[n])
            left_out[n] = rounded(part)
            copies += (
                send(left_out.at[n], left_in.at[n], l_send.at[n], l_recv.at[n], hub, sec),
            )
        finish(copies + (occ,))

    @pl.when(seg == last)
    def _():
        edges = edge_load(right_hbm)
        for step in range(1, sec_count):
            greet(last, turned(step))
        greet(last - 1, sec)
        greet_hubs()
        load.start()
        edges.wait()
        load.wait()
        own = edge_rows()
        kept = jnp.where(
            lax.rem(rows16, 4) == 0, right_mul(own, mats[0]), right_mul(own, mats[3])
        )
        ends[0, 0] = rounded(kept)
        ends[0, 1] = own
        pl.semaphore_wait(barrier, 7)
        copies = ()
        for step in (2, 1, 3):
            copies += (
                send(
                    ends.at[0], ends.at[sec_count - step], ch_send.at[step],
                    z_recv.at[sec_count - step], seg, turned(step),
                ),
            )
        for place, to in ((1, up), (0, down)):
            copies += (
                send(
                    blocks_hbm.at[1:3], gath.at[place, 1:3], gath_send.at[place],
                    gath_recv.at[place], seg, to,
                ),
            )
        occ = send_occ()
        for slot in range(1, 4):
            arrived(ends.at[slot], z_recv.at[slot])
        arrived(gath.at[2], gath_recv.at[2])
        for place in range(2):
            arrived(gath.at[place, 1:3], gath_recv.at[place])
        bond7 = []
        for turn, ones, twos in (
            (0, mats[1], mats[2]), (1, gath[0, 1], gath[0, 2]), (-1, gath[1, 1], gath[1, 2])
        ):
            kept = ends[turn % 4, 0].astype(jnp.float32)
            parts = [
                kept,
                right_mul(ends[(turn + 1) % 4, 1], ones),
                right_mul(ends[(turn - 1) % 4, 1], twos),
                kept,
            ]
            bond7.append(rounded(pick(lax.rem(rows16, 4), parts)))
        parts = [right_mul(bond7[place], gath[2, n]) for n, place in enumerate((0, 1, 2, 0))]
        y_out[0] = rounded(pick(lax.div(rows16, 4), parts))
        finish(copies)
        finish(to_all(y_out.at[0], hub) + (occ,))

    @pl.when(seg == 6)
    def _():
        greet_hubs()
        pl.semaphore_wait(barrier, 2)
        copy = send(blocks_hbm, gath.at[2], gath_send.at[0], gath_recv.at[2], last, sec)
        occ = send_occ()
        finish((copy, occ))

    @pl.when(seg == 5)
    def _():
        greet_hubs()
        pl.semaphore_wait(barrier, 3)
        copies = (
            send(blocks_hbm, gath.at[2], gath_send.at[1], gath_recv.at[2], hub, up),
            send(blocks_hbm, gath.at[1], gath_send.at[2], gath_recv.at[1], hub, down),
            send(blocks_hbm, gath.at[0], gath_send.at[0], gath_recv.at[0], hub, sec),
        )
        occ = send_occ()
        finish(copies + (occ,))

    @pl.when(seg == hub)
    def _():
        for step in (2, 1, 3, 0):
            greet(last, turned(step))
        greet(0, sec)
        for place in (up, down, sec):
            greet(hub + 1, place)
        for i in (1, 2, 3, last - 1):
            greet(i, sec)
        for step in range(1, sec_count):
            greet(hub, turned(step))
        load.start()
        own_occ = pltpu.make_async_copy(occ_hbm, occ_in.at[hub], occ_sem)
        own_occ.start()
        start = pltpu.make_async_copy(start_hbm, start_in, start_sem)
        start.start()
        own_occ.wait()
        start.wait()
        for i in range(seg_count):
            if i != hub:
                arrived(occ_in.at[i], occ_recv.at[i])
        occ = [occ_in[i] for i in range(seg_count)]
        middle = start_in[...]
        for n in occ[:half]:
            middle = middle + jnp.where(n == 1, 1, 0) - jnp.where(n == 2, 1, 0)
        key_l = occ[3] * 64 + occ[2] * 16 + occ[1] * 4 + occ[0]
        key_l = jnp.where(lax.rem(middle + 2 * sec_count, sec_count) == sec, key_l, -1)
        key_r = occ[4] * 64 + occ[5] * 16 + occ[6] * 4 + occ[7]
        rows = lax.broadcasted_iota(jnp.int32, (256, 128), 0)
        for j in range(8):
            here = slice(j * 128, (j + 1) * 128)
            one_r[:, here] = rounded(jnp.where(rows == key_r[j:j + 1, :], 1.0, 0.0))
            one_l[:, here] = rounded(jnp.where(rows == key_l[j:j + 1, :], 1.0, 0.0))
        load.wait()

        def select(vectors, one_hot):
            return lax.dot_general(
                vectors, one_hot[...], (((0,), (0,)), ((), ())),
                preferred_element_type=jnp.float32,
            )

        for place in range(3):
            arrived(gath.at[place], gath_recv.at[place])
        for slot in range(4):
            arrived(z_in.at[slot], z_recv.at[slot])
        bond6 = [z_in[slot] for slot in range(4)]
        bond5 = []
        for place, turn in enumerate((0, 1, -1)):
            parts = [
                rounded(right_mul(bond6[(turn + CHARGE[n]) % 4], gath[place, n]))
                for n in range(4)
            ]
            bond5.append(jnp.concatenate(parts, axis=0))
        right = jnp.concatenate([rounded(part) for part in right_products(bond5)], axis=0)
        sel_r[...] = select(right, one_r)
        for n in range(4):
            arrived(left_in.at[n], l_recv.at[n])
        left = jnp.concatenate([left_in[n] for n in range(4)], axis=0)
        value = jnp.sum(select(left, one_l) * sel_r[...], axis=0, keepdims=True)
        for j in range(8):
            part[j:j + 1, :] = value[:, j * 128:(j + 1) * 128]
        count = seg_count * sec_count
        pl.semaphore_wait(barrier, count - 1)
        copies = ()
        own = pltpu.make_async_copy(part, fin.at[sec], occ_sem)

        def spread(seg_to, sec_to):
            return (
                send(
                    part, fin.at[sec], fin_send.at[len(copies)], fin_recv.at[sec],
                    seg_to, sec_to,
                ),
            )

        for j in range(sec_count):
            place = jnp.where(sec < sec_count // 2, sec_count - 1 - j, j)
            for i in range(seg_count):
                if i != hub:
                    copies += spread(i, place)
            if j > 0:
                copies += spread(hub, turned(j))
        own.start()
        finish(copies)
        own.wait()

    for place in range(sec_count):
        @pl.when(jnp.logical_or(seg != hub, sec != place))
        def _():
            arrived(fin.at[place], fin_recv.at[place])


def tree_device(blocks, left_edge, right_edge, occupation, start_sector):
    seg_count = lax.axis_size("seg")
    sec_count = lax.axis_size("sec")
    hbm = pl.BlockSpec(memory_space=pl.ANY)
    dma = pltpu.SemaphoreType.DMA
    bf16, f32, i32 = jnp.bfloat16, jnp.float32, jnp.int32
    values = pl.pallas_call(
        functools.partial(tree_kernel, seg_count, sec_count),
        out_shape=jax.ShapeDtypeStruct((sec_count, 8, 128), f32),
        in_specs=[hbm] * 5,
        out_specs=hbm,
        scratch_shapes=[
            pltpu.VMEM((4, 128, 128), bf16),
            pltpu.VMEM((4, 4, 128, 128), bf16),
            pltpu.VMEM((2, 128, 128), bf16),
            pltpu.VMEM((4, 16, 128), bf16),
            pltpu.VMEM((4, 16, 128), bf16),
            pltpu.VMEM((4, 16, 128), bf16),
            pltpu.VMEM((4, 64, 128), bf16),
            pltpu.VMEM((4, 64, 128), bf16),
            pltpu.VMEM((1, 128), bf16),
            pltpu.VMEM((4, 2, 16, 128), bf16),
            pltpu.VMEM((8, 8, 128), i32),
            pltpu.VMEM((8, 128), i32),
            pltpu.VMEM((256, 1024), bf16),
            pltpu.VMEM((256, 1024), bf16),
            pltpu.VMEM((128, 1024), f32),
            pltpu.VMEM((8, 128), f32),
            dma, dma, dma, dma,
            dma((4,)),
            dma((3,)),
            dma((4,)),
            dma((6,)),
            dma((6,)),
            dma((4,)),
            dma((4,)),
            dma,
            dma((8,)),
            dma((seg_count * sec_count - 1,)),
            dma((4,)),
        ],
        compiler_params=pltpu.CompilerParams(
            collective_id=0, has_side_effects=True, vmem_limit_bytes=60 * 1024 * 1024
        ),
    )(
        blocks.reshape(4, 128, 128),
        left_edge,
        right_edge,
        occupation.reshape(8, 128),
        start_sector.reshape(8, 128),
    )
    return ((values[0] + values[1]) + (values[2] + values[3])).reshape(1024)


def fits_tree(mesh, blocks, occupation):
    seg_count, sec_count = mesh.shape["seg"], mesh.shape["sec"]
    return (
        seg_count == 8
        and sec_count == 4
        and blocks.shape == (8, 4, 4, 128, 128)
        and occupation.shape == (1024, 8)
    )


def padded_2(block, sides, width, periodic):
    for axis, dim in sides:
        count = lax.axis_size(axis)
        forward = [(i, i + 1) for i in range(count - 1)]
        if periodic:
            forward.append((count - 1, 0))
        backward = [(target, source) for source, target in forward]
        low = lax.ppermute(
            lax.slice_in_dim(block, block.shape[dim] - width, None, axis=dim), axis, forward
        )
        high = lax.ppermute(lax.slice_in_dim(block, 0, width, axis=dim), axis, backward)
        block = jnp.concatenate([low, block, high], axis=dim)
    return block


def state_masks(occ_site):
    levels = jnp.arange(4, dtype=jnp.int32)
    return (occ_site[:, None] == levels[None, :]).astype(jnp.float32)


def forward_send(vector, block_site, occ_masks):
    products = jnp.einsum("ka,nab->knb", vector, block_site, preferred_element_type=jnp.float32)
    terms = products * occ_masks[:, :, None]
    kept_term = (terms[:, 0] + terms[:, 3]).astype(jnp.bfloat16)
    upward = terms[:, 1].astype(jnp.bfloat16)
    downward = terms[:, 2].astype(jnp.bfloat16)
    return (kept_term, jnp.stack([downward, upward]))


def backward_send(vector, block_site, occ_masks):
    return (vector, jnp.stack([vector, vector]))


def forward_take(kept_term, padded, block_site, occ_masks):
    total = (
        kept_term.astype(jnp.float32)
        + padded[0].astype(jnp.float32)
        + padded[3].astype(jnp.float32)
    )
    return total.astype(jnp.bfloat16)


def backward_take(kept_term, padded, block_site, occ_masks):
    stacked = jnp.stack([kept_term, padded[3], padded[0], kept_term], axis=1)
    products = jnp.einsum("nab,knb->kna", block_site, stacked, preferred_element_type=jnp.float32)
    return jnp.sum(products * occ_masks[:, :, None], axis=1).astype(jnp.bfloat16)


def per_device(blocks, left_edge, right_edge, occupation, start_sector):
    seg_count = lax.axis_size("seg")
    half_count = seg_count // 2
    seg_index = lax.axis_index("seg")
    sec_index = lax.axis_index("sec")
    is_left = seg_index < half_count
    chain_depth = jnp.where(is_left, seg_index, seg_count - 1 - seg_index)
    is_first = chain_depth == 0
    meet_lower = seg_index == half_count - 1
    meet_upper = seg_index == half_count
    conf_count = occupation.shape[0]
    sites_here = occupation.shape[1]
    sector_width = blocks.shape[-1]
    block_count = 1
    columns = jnp.arange(sector_width, dtype=jnp.int32)
    lower_cols = (columns < sector_width // 2).astype(jnp.float32)
    upper_cols = 1.0 - lower_cols
    local_blocks = blocks[:, :, 0]
    left_row = left_edge[0]
    right_row = right_edge[0]
    batch_rows = conf_count // block_count

    def initial():
        zero_row = jnp.zeros_like(left_row)
        initial_left = jnp.where(
            (start_sector == sec_index)[:, None], left_row[None, :], zero_row[None, :]
        )
        initial_right = jnp.broadcast_to(right_row[None, :], (batch_rows, sector_width))
        return jnp.where(is_left, initial_left, initial_right)

    def run_sites(vector):
        position = jnp.where(is_left, 0, sites_here - 1)
        block_site = lax.dynamic_index_in_dim(local_blocks, position, 0, keepdims=False)
        occ_site = lax.dynamic_index_in_dim(occupation, position, 1, keepdims=False)
        occ_masks = state_masks(occ_site)
        kept_term, outgoing = lax.cond(
            is_left, forward_send, backward_send, vector, block_site, occ_masks
        )
        padded = padded_2(outgoing, (("sec", 0),), 1, True)
        vector = lax.cond(
            is_left, forward_take, backward_take, kept_term, padded, block_site, occ_masks
        )
        return vector

    section_count = half_count + block_count - 1

    def section(section_index, state_pair):
        incoming, partial_value = state_pair
        batch_index = section_index - chain_depth
        is_valid = (batch_index >= 0) & (batch_index < block_count)
        vector = jnp.where(is_first, initial(), incoming)
        vector = run_sites(vector)
        padded = padded_2(vector[None], (("seg", 0),), 1, False)
        received = jnp.where(is_left, padded[0], padded[2])
        own_vals = vector.astype(jnp.float32)
        lower_part = jnp.sum(own_vals * padded[2].astype(jnp.float32) * lower_cols[None, :], axis=1)
        upper_part = jnp.sum(own_vals * padded[0].astype(jnp.float32) * upper_cols[None, :], axis=1)
        product = jnp.where(meet_lower, lower_part, upper_part)
        previous = partial_value
        store_here = (meet_lower | meet_upper) & is_valid
        partial_value = jnp.where(store_here, product, previous)
        return (received, partial_value)

    start_state = (
        jnp.zeros((batch_rows, sector_width), jnp.bfloat16),
        jnp.zeros((conf_count,), jnp.float32),
    )
    final_state = lax.fori_loop(0, section_count, section, start_state)
    return lax.psum(final_state[1], ("seg", "sec"))


def solution(mesh):
    in_specs = (
        P("seg", None, "sec", None, None),
        P("sec", None),
        P("sec", None),
        P(None, "seg"),
        P(),
    )

    def run(blocks, left_edge, right_edge, occupation, start_sector):
        body = tree_device if fits_tree(mesh, blocks, occupation) else per_device
        return jax.shard_map(
            body, mesh=mesh, in_specs=in_specs, out_specs=P(), check_vma=False
        )(blocks, left_edge, right_edge, occupation, start_sector)

    return run
```
